512 devices in a mesh: src: 16 (over z), tgt: 32 (over x, y, core).
Axes of the slice: x: 4, y: 4, z: 16, core: 2. Of those that a mesh axis runs over, the one named last changes fastest.
Arguments:
- src_points: bfloat16 [16, 8192, 256], P('src', 'tgt'), may hold values from -4 to 4
- src_logmass: bfloat16 [16, 8192], P('src', 'tgt'), may hold values from -1 to 1
- tgt_points: bfloat16 [32, 4096, 256], P('tgt', 'src'), may hold values from -4 to 4
- tgt_logmass: bfloat16 [32, 4096], P('tgt', 'src'), may hold values from -1 to 1
- tile_list: int32 [16, 32, 80, 2], P('src', 'tgt'), may hold values from 0 to 63, as said below
- tile_count: int32 [16, 32], P('src', 'tgt'), may hold values from 64 to 80, as said below
Outputs:
- src_potential: float32 [16, 8192], P('src', 'tgt')
- tgt_potential: float32 [32, 4096], P('tgt', 'src')
The draws below stay inside these ranges and needn't reach their ends.
Inputs may be any that keep to these rules, and one draw needn't show every extreme that they name: `tile_list`: live slots hold distinct pairs (row tile, column tile) with row tile below 64 and column tile below 32; slot r < 64 holds (r, r mod 32); slots at or beyond the count hold (0, 0). `tile_count`: at most 80; exactly 80 for some block pair in every draw.
All inputs are finite; a program needn't handle non-finite values.
Results may differ from the reference program's by a relative error of at most 0.02.
Values may be sent and summed in bfloat16 or wider, within the bound.
A program may use at most 64 MiB of HBM per device.

```python
import jax
import jax.numpy as jnp
from jax import lax

D = 256
TILE = 128
ROW_TILES = 64
COL_TILES = 32
SLOTS = 80
ITERS = 3
SRC_ROWS = 8192
TGT_ROWS = 4096
N_SRC = 16
N_TGT = 32


point_scale = 2.5


def draw_src_points(key, part):
    shape = (N_SRC, ROW_TILES * TILE, D)
    base = jax.random.normal(jax.random.fold_in(key, 1), shape, jnp.float32) * (point_scale / jnp.sqrt(float(D)))
    return jnp.clip(base, -4.0, 4.0).astype(jnp.bfloat16)


def draw_tgt_points(key, part):
    shape = (N_TGT, COL_TILES * TILE, D)
    base = jax.random.normal(jax.random.fold_in(key, 3), shape, jnp.float32) * (point_scale / jnp.sqrt(float(D)))
    return jnp.clip(base, -4.0, 4.0).astype(jnp.bfloat16)


def kept_tiles(key):
    devices = N_SRC * N_TGT
    pairs = ROW_TILES * COL_TILES
    index = jnp.arange(pairs, dtype=jnp.int32)
    tile_rows = index // COL_TILES
    tile_cols = index % COL_TILES
    cover = tile_cols == tile_rows % COL_TILES

    def one_device(device_key):
        ranks = jax.random.permutation(device_key, pairs).astype(jnp.int32)
        score = jnp.where(cover, index - 2 * pairs, ranks)
        order = jnp.argsort(score)[:SLOTS]
        return (tile_rows[order], tile_cols[order])
    keys = jax.random.split(jax.random.fold_in(key, 11), devices)
    chosen_rows, chosen_cols = jax.vmap(one_device)(keys)
    spread = SLOTS - ROW_TILES
    draws = jax.random.randint(jax.random.fold_in(key, 12), (3, devices), 0, spread + 1)
    counts = ROW_TILES + jnp.min(draws, axis=0)
    fullest = jax.random.randint(jax.random.fold_in(key, 13), (), 0, devices)
    counts = jnp.where(jnp.arange(devices) == fullest, SLOTS, counts).astype(jnp.int32)
    live = jnp.arange(SLOTS)[None, :] < counts[:, None]
    chosen_rows = jnp.where(live, chosen_rows, 0)
    chosen_cols = jnp.where(live, chosen_cols, 0)
    listing = jnp.stack([chosen_rows, chosen_cols], axis=-1).astype(jnp.int32)
    return (listing.reshape(N_SRC, N_TGT, SLOTS, 2), counts.reshape(N_SRC, N_TGT))


def draw_tile_list(key, part):
    return kept_tiles(key)[0]


def draw_tile_count(key, part):
    return kept_tiles(key)[1]


def level_of(stream_key, shape, cuts, low, top_value):
    def one(axis_at, parts):
        steps = jax.random.uniform(jax.random.fold_in(jax.random.fold_in(stream_key, 6), axis_at), (parts,), jnp.float32, low / len(cuts), top_value / len(cuts))
        return jnp.repeat(jnp.exp(steps), shape[axis_at] // parts).reshape((-1,) + (1,) * (len(shape) - axis_at - 1))

    gain = one(*cuts[0])
    for cut in cuts[1:]:
        gain = gain * one(*cut)
    return gain


def setup_inputs(seed: int = 0) -> dict:
    key_list = jax.random.split(jax.random.key(seed), 7)
    return {
        "src_points": draw_src_points(jax.random.fold_in(key_list[6], 71), 0),
        "src_logmass": jnp.clip(jax.random.uniform(key_list[1], (N_SRC, SRC_ROWS), jnp.float32, -1.0, 1.0) * level_of(key_list[1], (N_SRC, SRC_ROWS), ((0, 16), (1, 32)), -0.4, 0.0), -1.0, 1.0).astype(jnp.bfloat16),
        "tgt_points": draw_tgt_points(jax.random.fold_in(key_list[6], 71), 0),
        "tgt_logmass": jnp.clip(jax.random.uniform(key_list[3], (N_TGT, TGT_ROWS), jnp.float32, -1.0, 1.0) * level_of(key_list[3], (N_TGT, TGT_ROWS), ((0, 32), (1, 16)), -0.4, 0.0), -1.0, 1.0).astype(jnp.bfloat16),
        "tile_list": draw_tile_list(jax.random.fold_in(key_list[6], 71), 0),
        "tile_count": draw_tile_count(jax.random.fold_in(key_list[6], 71), 0),
    }


inverse_eps = 20.0
lowest_log = -1.0e30


def block_costs(source_tiles, target_tiles, src_index, tgt_index, row_ids, col_ids):
    left_rows = source_tiles[src_index[:, None], row_ids].astype(jnp.float32)
    right_rows = target_tiles[tgt_index[:, None], col_ids].astype(jnp.float32)
    products = jnp.einsum("psad,psbd->psab", left_rows, right_rows, precision=lax.Precision.HIGHEST)
    return (1.0 - products).astype(jnp.bfloat16)


def gather_lse(peak, summed, owners):
    highest = jnp.where(owners[..., None], peak[:, :, None, :], lowest_log).max(axis=(0, 1))
    shortfall = jnp.minimum(peak[:, :, None, :] - highest[None, None], 0.0)
    added = jnp.where(owners[..., None], summed[:, :, None, :] * jnp.exp(shortfall), 0.0).sum(axis=(0, 1))
    return highest + jnp.log(added)


def reference(src_points, src_logmass, tgt_points, tgt_logmass, tile_list, tile_count):
    features = src_points.shape[2]
    source_tiles = src_points.reshape(N_SRC, ROW_TILES, TILE, features)
    target_tiles = tgt_points.reshape(N_TGT, COL_TILES, TILE, features)
    live_slots = jnp.arange(SLOTS, dtype=jnp.int32)[None, None, :] < tile_count[:, :, None]
    row_range = jnp.arange(ROW_TILES, dtype=jnp.int32)
    col_range = jnp.arange(COL_TILES, dtype=jnp.int32)
    every_src = jnp.arange(N_SRC, dtype=jnp.int32)
    every_tgt = jnp.arange(N_TGT, dtype=jnp.int32)

    def row_update(column_pot):
        def per_source(index):
            row_ids = tile_list[index, :, :, 0]
            col_ids = tile_list[index, :, :, 1]
            tile_cost = block_costs(source_tiles, target_tiles, jnp.full((N_TGT,), index, jnp.int32), every_tgt, row_ids, col_ids)
            scores = column_pot[every_tgt[:, None], col_ids][:, :, None, :] - inverse_eps * tile_cost.astype(jnp.float32)
            peak = scores.max(axis=3)
            summed = jnp.exp(scores - peak[..., None]).sum(axis=3)
            owners = (row_ids[..., None] == row_range) & live_slots[index][..., None]
            return src_logmass[index].astype(jnp.float32) - gather_lse(peak, summed, owners).reshape(-1)
        return lax.map(per_source, every_src)

    def col_update(row_pot):
        def per_target(index):
            row_ids = tile_list[:, index, :, 0]
            col_ids = tile_list[:, index, :, 1]
            tile_cost = block_costs(source_tiles, target_tiles, every_src, jnp.full((N_SRC,), index, jnp.int32), row_ids, col_ids)
            scores = row_pot[every_src[:, None], row_ids][:, :, :, None] - inverse_eps * tile_cost.astype(jnp.float32)
            peak = scores.max(axis=2)
            summed = jnp.exp(scores - peak[:, :, None, :]).sum(axis=2)
            owners = (col_ids[..., None] == col_range) & live_slots[:, index][..., None]
            return tgt_logmass[index].astype(jnp.float32) - gather_lse(peak, summed, owners).reshape(-1)
        return lax.map(per_target, every_tgt)

    column_pot = jnp.zeros((N_TGT, COL_TILES, TILE), jnp.float32)
    row_pot = jnp.zeros((N_SRC, ROW_TILES, TILE), jnp.float32)
    for sweep in range(ITERS):
        row_pot = row_update(column_pot).reshape(N_SRC, ROW_TILES, TILE)
        column_pot = col_update(row_pot).reshape(N_TGT, COL_TILES, TILE)
    return row_pot.reshape(N_SRC, ROW_TILES * TILE), column_pot.reshape(N_TGT, COL_TILES * TILE)
```

```python
import math

import jax
import jax.numpy as jnp
from jax import lax
from jax.experimental import pallas as pl
from jax.experimental.pallas import tpu as pltpu
from jax.sharding import PartitionSpec as P

MESH = pl.DeviceIdType.MESH
TILE = 128
D = 256
ROW_TILES = 64
COL_TILES = 32
SLOTS = 80
FIXED = 64
EXTRA = SLOTS - FIXED
ITERS = 3
NS = 16
NT = 32
CHIPS = 16
HALF = ROW_TILES // 2
LOG2E = math.log2(math.e)
LN2 = math.log(2.0)
SCALE = -20.0 * LOG2E
LOWEST = -1.0e30
NT_DIMS = (((1,), (1,)), ((), ()))


def scaled_cost(left, right):
    products = lax.dot_general(left, right, NT_DIMS, preferred_element_type=jnp.float32)
    return (1.0 - products).astype(jnp.bfloat16).astype(jnp.float32) * SCALE


def peak_and_sum(scores):
    peak = jnp.max(scores, axis=0, keepdims=True)
    return peak, jnp.sum(jnp.exp2(scores - peak), axis=0, keepdims=True)


def lse_leading(parts):
    peak = jnp.max(parts, axis=0)
    return peak + jnp.log2(jnp.sum(jnp.exp2(parts - peak[None]), axis=0))


def kernel(
    xp, am, yp, bm, tiles, count, s_out, t_out,
    X, Y, A, AT, a_parts, b_parts, a_all, b_all, own_a, own_b,
    peak_r, sum_r, peak_x, sum_x, s_pot, t_pot, l_row, half_in, half_out, row_in,
    col_out, col_in, fin_out, fin_in,
    z_up, z_dn, z_send, x_recv, sib_recv, x_send, mass_recv, mass_send,
    half_recv, half_send, row_recv, row_send, col_recv, col_send,
):
    i = lax.axis_index("src")
    k = lax.axis_index("tgt")
    chip = k // 2
    core = lax.rem(k, 2)
    sibling = k + 1 - 2 * core
    up = lax.rem(i + 1, NS)
    dn = lax.rem(i + NS - 1, NS)

    barrier = pltpu.get_barrier_semaphore()

    def greet_plane(d, c):
        pl.semaphore_signal(barrier, inc=1, device_id=(i, lax.rem(k + d, NT)), device_id_type=MESH)
        return c

    def greet_line(d, c):
        pl.semaphore_signal(barrier, inc=1, device_id=(lax.rem(i + d, NS), k), device_id_type=MESH)
        return c

    lax.fori_loop(1, NT, greet_plane, 0)
    lax.fori_loop(1, NS, greet_line, 0)
    pl.semaphore_wait(barrier, NT - 1 + NS - 1)

    def remote(src, dst, ssem, rsem, dev):
        return pltpu.make_async_remote_copy(
            src_ref=src, dst_ref=dst, send_sem=ssem, recv_sem=rsem, device_id=dev, device_id_type=MESH
        )

    def drain(like, sem):
        pltpu.make_async_copy(like, like, sem).wait()

    def z_copy(src, shard, q, step, direction):
        tile = 2 * shard + q // 2
        dst = Y.at[tile, lax.rem(q, 2)]
        if src is None:
            src = dst
        if direction == 0:
            return remote(src, dst, z_send.at[0], z_up.at[step * 4 + q], (up, k))
        return remote(src, dst, z_send.at[1], z_dn.at[step * 4 + q], (dn, k))

    for q in range(4):
        for direction in range(2):
            z_copy(yp.at[q // 2, pl.ds((q % 2) * 64, 64)], i, q, 0, direction).start()
    sib_dev = (i, sibling)
    remote(xp, X.at[pl.ds(2 * k, 2)], x_send.at[1], sib_recv.at[0], sib_dev).start()

    def send_x(d, c):
        to = 2 * lax.rem(chip + d, CHIPS) + core
        remote(xp, X.at[pl.ds(2 * k, 2)], x_send.at[0], x_recv.at[d], (i, to)).start()
        return c

    lax.fori_loop(1, CHIPS, send_x, 0)

    own_a[0:1, :] = am[:, 0:TILE].astype(jnp.float32) * LOG2E
    own_a[1:2, :] = am[:, TILE:].astype(jnp.float32) * LOG2E
    own_b[0:1, :] = bm[:, 0:TILE].astype(jnp.float32) * LOG2E
    own_b[1:2, :] = bm[:, TILE:].astype(jnp.float32) * LOG2E

    def send_a(d, c):
        remote(own_a, a_parts.at[k], mass_send.at[0], mass_recv.at[0], (i, lax.rem(k + d, NT))).start()
        return c

    def send_b(d, c):
        remote(own_b, b_parts.at[i], mass_send.at[1], mass_recv.at[1], (lax.rem(i + d, NS), k)).start()
        return c

    lax.fori_loop(1, NT, send_a, 0)
    lax.fori_loop(1, NS, send_b, 0)
    a_parts[k] = own_a[...]
    b_parts[i] = own_b[...]
    X[pl.ds(2 * k, 2)] = xp[...]
    Y[pl.ds(2 * i, 2)] = yp[...].reshape(2, 2, 64, D)

    def serve_x(d):
        theirs = 2 * lax.rem(chip + CHIPS - d, CHIPS) + core
        block = X.at[pl.ds(2 * theirs, 2)]
        drain(block, x_recv.at[d])
        remote(block, block, x_send.at[1], sib_recv.at[d], sib_dev).start()

    def wait_sib(d, c):
        theirs = 2 * lax.rem(chip + CHIPS - d, CHIPS) + 1 - core
        block = X.at[pl.ds(2 * theirs, 2)]
        drain(block, sib_recv.at[d])
        return c

    def ring_step(step, c):
        lo = lax.rem(i + NS - step, NS)
        hi = lax.rem(i + step, NS)
        for q in range(4):
            for direction, shard in ((0, lo), (1, hi)):
                mine = Y.at[2 * shard + q // 2, q % 2]
                sem = (z_up, z_dn)[direction].at[(step - 1) * 4 + q]
                drain(mine, sem)
                z_copy(None, shard, q, step, direction).start()
        serve_x(2 * step - 1)
        serve_x(2 * step)
        return c

    lax.fori_loop(1, 7, ring_step, 0)
    lo = lax.rem(i + NS - 7, NS)
    hi = lax.rem(i + 7, NS)
    for q in range(4):
        for direction, shard in ((0, lo), (1, hi)):
            drain(Y.at[2 * shard + q // 2, q % 2], (z_up, z_dn)[direction].at[6 * 4 + q])
            if q // 2 == direction:
                z_copy(None, shard, q, 7, direction).start()
    for d in (13, 14, 15):
        serve_x(d)
    far = lax.rem(i + 8, NS)
    for q in range(4):
        drain(Y.at[2 * far + q // 2, q % 2], (z_up, z_dn)[q // 2].at[7 * 4 + q])
    lax.fori_loop(0, CHIPS, wait_sib, 0)
    drain(a_parts.at[pl.ds(0, NT - 1)], mass_recv.at[0])
    drain(b_parts.at[pl.ds(0, NS - 1)], mass_recv.at[1])

    def lay_a(n, c):
        for h in range(2):
            a_all[pl.ds(2 * n + h, 1), :] = a_parts[n, h : h + 1]
        return c

    def lay_b(n, c):
        for h in range(2):
            b_all[pl.ds(2 * n + h, 1), :] = b_parts[n, h : h + 1]
        return c

    lax.fori_loop(0, NT, lay_a, 0)
    lax.fori_loop(0, NS, lay_b, 0)

    def fixed_tiles(c, carry):
        y = Y[c].reshape(TILE, D)
        for h in range(2):
            r = c + COL_TILES * h
            x = X[r]
            costs = scaled_cost(y, x)
            AT[r] = costs
            peak, total = peak_and_sum(costs)
            peak_r[pl.ds(r, 1), :] = peak
            sum_r[pl.ds(r, 1), :] = total
            A[r] = scaled_cost(x, y)
        return carry

    lax.fori_loop(0, COL_TILES, fixed_tiles, 0)

    live_count = count[0]

    def alive(s):
        return jnp.full((1, TILE), live_count, jnp.int32) > FIXED + s

    def keep_extra(s, peak, total):
        peak_x[pl.ds(s, 1), :] = jnp.where(alive(s), peak, LOWEST)
        sum_x[pl.ds(s, 1), :] = total

    def extra_tiles(s, carry):
        x = X[tiles[2 * (FIXED + s)]]
        y = Y[tiles[2 * (FIXED + s) + 1]].reshape(TILE, D)
        costs = scaled_cost(y, x)
        AT[FIXED + s] = costs
        keep_extra(s, *peak_and_sum(costs))
        A[FIXED + s] = scaled_cost(x, y)
        return carry

    lax.fori_loop(0, EXTRA, extra_tiles, 0)

    def fold(peak, total, which):
        owner = lax.broadcasted_iota(jnp.int32, peak.shape, 0)
        px = peak_x[...]
        sx = sum_x[...]
        highest = peak
        for s in range(EXTRA):
            mine = owner == tiles[2 * (FIXED + s) + which]
            highest = jnp.maximum(highest, jnp.where(mine, px[s : s + 1], LOWEST))
        total = total * jnp.exp2(peak - highest)
        for s in range(EXTRA):
            mine = owner == tiles[2 * (FIXED + s) + which]
            shortfall = jnp.minimum(px[s : s + 1] - highest, 0.0)
            total = total + jnp.where(mine, sx[s : s + 1] * jnp.exp2(shortfall), 0.0)
        return highest + jnp.log2(total)

    def columns_of(pot):
        rows = pot.shape[0]
        full = jnp.concatenate([pot, jnp.zeros((TILE - rows, TILE), jnp.float32)], axis=0)
        return full.T

    def pick(cols, n):
        lane = lax.broadcasted_iota(jnp.int32, (TILE, TILE), 1)
        return jnp.sum(jnp.where(lane == n, cols, 0.0), axis=1, keepdims=True)

    def row_pass():
        cols = columns_of(t_pot[...])

        def group(g, carry):
            near = pltpu.roll(cols, lax.rem(TILE - 8 * g, TILE), 1)
            for u in range(8):
                pot = near[:, u : u + 1]
                for h in range(2):
                    r = 8 * g + u + COL_TILES * h
                    peak, total = peak_and_sum(AT[r] + pot)
                    peak_r[pl.ds(r, 1), :] = peak
                    sum_r[pl.ds(r, 1), :] = total
            return carry

        lax.fori_loop(0, COL_TILES // 8, group, 0)

        def extra(s, carry):
            pot = pick(cols, tiles[2 * (FIXED + s) + 1])
            keep_extra(s, *peak_and_sum(AT[FIXED + s] + pot))
            return carry

        lax.fori_loop(0, EXTRA, extra, 0)

    def col_pass():
        cols = columns_of(s_pot[...])

        def group(g, carry):
            near = pltpu.roll(cols, lax.rem(TILE - 8 * g, TILE), 1)
            for u in range(8):
                c = 8 * g + u
                first = A[c] + near[:, u : u + 1]
                second = A[c + COL_TILES] + near[:, COL_TILES + u : COL_TILES + u + 1]
                peak, total = peak_and_sum(jnp.concatenate([first, second], axis=0))
                peak_r[pl.ds(c, 1), :] = peak
                sum_r[pl.ds(c, 1), :] = total
            return carry

        lax.fori_loop(0, COL_TILES // 8, group, 0)

        def extra(s, carry):
            pot = pick(cols, tiles[2 * (FIXED + s)])
            keep_extra(s, *peak_and_sum(A[FIXED + s] + pot))
            return carry

        lax.fori_loop(0, EXTRA, extra, 0)

    for it in range(ITERS):
        if it > 0:
            row_pass()
        logs = fold(peak_r[...], sum_r[...], 0)
        l_row[it] = logs.reshape(2, HALF, TILE)
        remote(l_row.at[it, 1 - core], half_in.at[it], half_send.at[it], half_recv.at[it], sib_dev).start()
        drain(half_in.at[it], half_recv.at[it])
        one, two = l_row[it, core], half_in[it]
        top = jnp.maximum(one, two)
        both = top + jnp.log2(jnp.exp2(one - top) + jnp.exp2(two - top))
        half_out[it] = both
        row_in[it, k] = both

        def send_row(d, c):
            remote(
                half_out.at[it], row_in.at[it, k], row_send.at[it], row_recv.at[it], (i, lax.rem(k + d, NT))
            ).start()
            return c

        lax.fori_loop(1, NT, send_row, 0)
        drain(row_in.at[it, pl.ds(0, NT - 1)], row_recv.at[it])
        total = lse_leading(row_in[it].reshape(CHIPS, ROW_TILES, TILE))
        s_pot[...] = a_all[...] - total

        col_pass()
        logs = fold(peak_r[0:COL_TILES, :], sum_r[0:COL_TILES, :], 1)
        if it + 1 < ITERS:
            col_out[it] = logs
            col_in[it, i] = logs

            def send_col(d, c):
                remote(
                    col_out.at[it], col_in.at[it, i], col_send.at[it], col_recv.at[it], (lax.rem(i + d, NS), k)
                ).start()
                return c

            lax.fori_loop(0, NS - 1, lambda d, c: send_col(lax.rem(d + 8, NS - 1) + 1, c), 0)
            drain(col_in.at[it, pl.ds(0, NS - 1)], col_recv.at[it])
            t_pot[...] = b_all[...] - lse_leading(col_in[it])
    for n in range(NS):
        fin_out[n] = logs[2 * n : 2 * n + 2]
    fin_in[i] = fin_out[i]

    def send_fin(d, c):
        to = lax.rem(i + lax.rem(d + 8, NS - 1) + 1, NS)
        remote(fin_out.at[to], fin_in.at[i], col_send.at[2], col_recv.at[2], (to, k)).start()
        return c

    lax.fori_loop(0, NS - 1, send_fin, 0)
    s_out[...] = s_pot[pl.ds(2 * k, 2), :] * LN2
    drain(Y.at[pl.ds(0, 15)], z_send.at[0])
    drain(Y.at[pl.ds(0, 15)], z_send.at[1])
    drain(X.at[pl.ds(0, 30)], x_send.at[0])
    drain(X.at[pl.ds(0, 32)], x_send.at[1])
    drain(a_parts.at[pl.ds(0, NT - 1)], mass_send.at[0])
    drain(b_parts.at[pl.ds(0, NS - 1)], mass_send.at[1])
    for it in range(ITERS):
        drain(half_in.at[it], half_send.at[it])
        drain(row_in.at[it, pl.ds(0, NT - 1)], row_send.at[it])
        if it + 1 < ITERS:
            drain(col_in.at[it, pl.ds(0, NS - 1)], col_send.at[it])
    drain(fin_in.at[pl.ds(0, NS - 1)], col_send.at[2])
    drain(fin_in.at[pl.ds(0, NS - 1)], col_recv.at[2])
    t_out[...] = (own_b[...] - lse_leading(fin_in[...])) * LN2


def shards(src_points, src_logmass, tgt_points, tgt_logmass, tile_list, tile_count):
    f32, bf16 = jnp.float32, jnp.bfloat16
    vmem = pl.BlockSpec(memory_space=pltpu.VMEM)
    smem = pl.BlockSpec(memory_space=pltpu.SMEM)
    dma = pltpu.SemaphoreType.DMA
    s, t = pl.pallas_call(
        kernel,
        out_shape=(
            jax.ShapeDtypeStruct((2, TILE), f32),
            jax.ShapeDtypeStruct((2, TILE), f32),
        ),
        in_specs=[vmem, vmem, vmem, vmem, smem, smem],
        out_specs=(vmem, vmem),
        scratch_shapes=[
            pltpu.VMEM((ROW_TILES, TILE, D), bf16),
            pltpu.VMEM((COL_TILES, 2, 64, D), bf16),
            pltpu.VMEM((SLOTS, TILE, TILE), f32),
            pltpu.VMEM((SLOTS, TILE, TILE), f32),
            pltpu.VMEM((NT, 2, TILE), f32),
            pltpu.VMEM((NS, 2, TILE), f32),
            pltpu.VMEM((ROW_TILES, TILE), f32),
            pltpu.VMEM((COL_TILES, TILE), f32),
            pltpu.VMEM((2, TILE), f32),
            pltpu.VMEM((2, TILE), f32),
            pltpu.VMEM((ROW_TILES, TILE), f32),
            pltpu.VMEM((ROW_TILES, TILE), f32),
            pltpu.VMEM((EXTRA, TILE), f32),
            pltpu.VMEM((EXTRA, TILE), f32),
            pltpu.VMEM((ROW_TILES, TILE), f32),
            pltpu.VMEM((COL_TILES, TILE), f32),
            pltpu.VMEM((ITERS, 2, HALF, TILE), f32),
            pltpu.VMEM((ITERS, HALF, TILE), f32),
            pltpu.VMEM((ITERS, HALF, TILE), f32),
            pltpu.VMEM((ITERS, NT, HALF, TILE), f32),
            pltpu.VMEM((ITERS - 1, COL_TILES, TILE), f32),
            pltpu.VMEM((ITERS - 1, NS, COL_TILES, TILE), f32),
            pltpu.VMEM((NS, 2, TILE), f32),
            pltpu.VMEM((NS, 2, TILE), f32),
            dma((32,)),
            dma((32,)),
            dma((2,)),
            dma((CHIPS,)),
            dma((CHIPS,)),
            dma((2,)),
            dma((2,)),
            dma((2,)),
            dma((ITERS,)),
            dma((ITERS,)),
            dma((ITERS,)),
            dma((ITERS,)),
            dma((ITERS,)),
            dma((ITERS,)),
        ],
        compiler_params=pltpu.CompilerParams(
            collective_id=0, has_side_effects=True, vmem_limit_bytes=50 * 2**20
        ),
    )(
        src_points.reshape(2, TILE, D),
        src_logmass,
        tgt_points.reshape(2, TILE, D),
        tgt_logmass,
        tile_list.reshape(2 * SLOTS),
        tile_count.reshape(1),
    )
    return s.reshape(1, 2 * TILE), t.reshape(1, 2 * TILE)


def solution(mesh):
    placed = (
        P("src", "tgt", None),
        P("src", "tgt"),
        P("tgt", "src", None),
        P("tgt", "src"),
        P("src", "tgt", None, None),
        P("src", "tgt"),
    )
    return jax.shard_map(
        shards,
        mesh=mesh,
        in_specs=placed,
        out_specs=(P("src", "tgt"), P("tgt", "src")),
        check_vma=False,
    )
```

```python
import math

import jax
import jax.numpy as jnp
from jax import lax
from jax.experimental import pallas as pl
from jax.experimental.pallas import tpu as pltpu
from jax.sharding import PartitionSpec as P

MESH = pl.DeviceIdType.MESH
TILE = 128
D = 256
ROW_TILES = 64
COL_TILES = 32
SLOTS = 80
FIXED = 64
EXTRA = SLOTS - FIXED
ITERS = 3
NS = 16
NT = 32
HALF = ROW_TILES // 2
LOG2E = math.log2(math.e)
LN2 = math.log(2.0)
SCALE = -20.0 * LOG2E
LOWEST = -1.0e30
NT_DIMS = (((1,), (1,)), ((), ()))


def scaled_cost(left, right):
    products = lax.dot_general(left, right, NT_DIMS, preferred_element_type=jnp.float32)
    return (1.0 - products).astype(jnp.bfloat16).astype(jnp.float32) * SCALE


def peak_and_sum(scores):
    peak = jnp.max(scores, axis=0, keepdims=True)
    return peak, jnp.sum(jnp.exp2(scores - peak), axis=0, keepdims=True)


def lse_leading(parts):
    peak = jnp.max(parts, axis=0)
    return peak + jnp.log2(jnp.sum(jnp.exp2(parts - peak[None]), axis=0))


def kernel(
    xp, am, yp, bm, tiles, count, s_out, t_out,
    X, Y, A, AT, a_parts, b_parts, a_all, b_all, own_a, own_b,
    peak_r, sum_r, peak_x, sum_x, s_pot, t_pot, row_tot, col_tot,
    half_out, half_in, row_out, row_in, row_out16, row_in16,
    col_out, col_in, col_out16, col_in16, fin_out, fin_in,
    z_up, z_dn, z_send, xa, xb, x_send, sib_recv, mass_recv, mass_send, local,
    half_recv, half_send, row_recv, row_send, col_recv, col_send,
):
    i = lax.axis_index("src")
    k = lax.axis_index("tgt")
    core = lax.rem(k, 2)
    sibling = k + 1 - 2 * core
    up = lax.rem(i + 1, NS)
    dn = lax.rem(i + NS - 1, NS)
    px, py = k // 8, lax.rem(k // 2, 4)
    pa = px * (1 - core) + py * core
    pb = py * (1 - core) + px * core

    def at(da, db):
        a, b = lax.rem(pa + 4 + da, 4), lax.rem(pb + 4 + db, 4)
        return (a * (1 - core) + b * core) * 8 + (b * (1 - core) + a * core) * 2 + core

    barrier = pltpu.get_barrier_semaphore()
    near = ((up, k), (dn, k), (i, at(1, 0)), (i, at(-1, 0)), (i, at(0, 1)), (i, at(0, -1)), (i, sibling))
    for dev in near:
        pl.semaphore_signal(barrier, inc=1, device_id=dev, device_id_type=MESH)
    own_x = pltpu.make_async_copy(xp, X.at[pl.ds(2 * k, 2)], local.at[0])
    own_y = pltpu.make_async_copy(yp, Y.at[pl.ds(2 * i, 2)], local.at[1])
    own_x.start()
    own_y.start()
    own_x.wait()
    own_y.wait()
    pl.semaphore_wait(barrier, len(near))

    def remote(src, dst, ssem, rsem, dev):
        return pltpu.make_async_remote_copy(
            src_ref=src, dst_ref=dst, send_sem=ssem, recv_sem=rsem, device_id=dev, device_id_type=MESH
        )

    def drain(like, sem):
        pltpu.make_async_copy(like, like, sem).wait()

    def z_copy(shard, q, step, direction):
        block = Y.at[2 * shard + q // 2, pl.ds((q % 2) * 64, 64)]
        if direction == 0:
            return remote(block, block, z_send.at[0], z_up.at[step * 4 + q], (up, k))
        return remote(block, block, z_send.at[1], z_dn.at[step * 4 + q], (dn, k))

    def z_wait(shard, q, step, direction):
        drain(Y.at[2 * shard + q // 2, pl.ds((q % 2) * 64, 64)], (z_up, z_dn)[direction].at[step * 4 + q])

    def x_block(da, db):
        return X.at[pl.ds(2 * at(da, db), 2)]

    def x_tile(da, db, t):
        return X.at[2 * at(da, db) + t]

    def x_copy(block, sem, da, db):
        remote(block, block, x_send.at[0], sem, (i, at(da, db))).start()

    def x_sibling(da, db):
        block = x_block(da, db)
        remote(block, block, x_send.at[1], sib_recv.at[0], (i, sibling)).start()

    OFFSETS = (0, -1, 1, 2)

    def x_both(j):
        block = x_block(OFFSETS[j], 0)
        x_copy(block, xb.at[j], 0, 1)
        x_copy(block, xb.at[4 + j], 0, -1)
        x_sibling(OFFSETS[j], 0)

    def x_step(step):
        if step == 1:
            for j, da, tile in ((1, -1, 0), (2, 1, 1)):
                drain(x_block(da, 0), xa.at[j - 1])
                x_copy(x_tile(da, 0, tile), xa.at[1 + j], -da, 0)
                x_both(j)
        if step == 2:
            drain(x_tile(2, 0, 0), xa.at[2])
            drain(x_tile(2, 0, 1), xa.at[3])
            x_both(3)
        for j in {2: (0,), 3: (1, 2), 4: (3,)}.get(step, ()):
            for n, db in ((0, -1), (1, 1)):
                drain(x_block(OFFSETS[j], db), xb.at[4 * n + j])
                x_copy(x_tile(OFFSETS[j], db, n), xb.at[8 + 4 * n + j], 0, -db)
                x_sibling(OFFSETS[j], db)
        for j in {4: (0,), 5: (1, 2, 3)}.get(step, ()):
            for n in range(2):
                drain(x_tile(OFFSETS[j], 2, n), xb.at[8 + 4 * n + j])
            x_sibling(OFFSETS[j], 2)
        if step == 6:
            drain(X.at[pl.ds(0, 2 * NS)], sib_recv.at[0])

    def shard_costs(n, carry):
        shard = lax.rem(i + n, NS)
        for half in range(2):
            c = 2 * shard + half
            y = Y[c]
            for h in range(2):
                r = c + COL_TILES * h
                costs = scaled_cost(y, X[r])
                AT[r] = costs
                peak, total = peak_and_sum(costs)
                peak_r[pl.ds(r, 1), :] = peak
                sum_r[pl.ds(r, 1), :] = total
        return carry

    for q in range(4):
        for direction in range(2):
            z_copy(i, q, 0, direction).start()
    x_copy(x_block(0, 0), xa.at[0], 1, 0)
    x_copy(x_block(0, 0), xa.at[1], -1, 0)
    x_both(0)
    own_a[0:1, :] = am[:, 0:TILE].astype(jnp.float32) * LOG2E
    own_a[1:2, :] = am[:, TILE:].astype(jnp.float32) * LOG2E
    own_b[0:1, :] = bm[:, 0:TILE].astype(jnp.float32) * LOG2E
    own_b[1:2, :] = bm[:, TILE:].astype(jnp.float32) * LOG2E
    a_parts[k] = own_a[...]
    b_parts[i] = own_b[...]
    for step in range(1, 8):
        lo = lax.rem(i + NS - step, NS)
        hi = lax.rem(i + step, NS)
        for q in range(4):
            for direction, shard in ((0, lo), (1, hi)):
                z_wait(shard, q, step - 1, direction)
                if step < 7 or q // 2 == direction:
                    z_copy(shard, q, step, direction).start()
        x_step(step)
        if step == 6:
            lax.fori_loop(NS - 3, NS + 4, shard_costs, 0)
        if step == 7:
            lax.fori_loop(NS - 6, NS - 3, shard_costs, 0)
            lax.fori_loop(4, 7, shard_costs, 0)
    far = lax.rem(i + 8, NS)
    for q in range(4):
        z_wait(far, q, 7, q // 2)
    lax.fori_loop(7, 10, shard_costs, 0)
    live_count = count[0, 0]

    def alive(s):
        return jnp.full((1, TILE), live_count, jnp.int32) > FIXED + s

    def keep_extra(s, peak, total):
        peak_x[pl.ds(s, 1), :] = jnp.where(alive(s), peak, LOWEST)
        sum_x[pl.ds(s, 1), :] = total

    def row_of(s):
        return tiles[0, FIXED + s]

    def col_of(s):
        return tiles[1, FIXED + s]

    def grouped(body, count, size):
        def group(g, carry):
            for u in range(size):
                body(size * g + u)
            return carry

        lax.fori_loop(0, count // size, group, 0)

    def extra_first(s):
        costs = scaled_cost(Y[col_of(s)], X[row_of(s)])
        AT[FIXED + s] = costs
        keep_extra(s, *peak_and_sum(costs))

    def extra_second(s):
        A[FIXED + s] = scaled_cost(X[row_of(s)], Y[col_of(s)])

    def fixed_second(c):
        for h in range(2):
            r = c + COL_TILES * h
            A[r] = scaled_cost(X[r], Y[c])

    def fold(first, which):
        peak = peak_r[pl.ds(first, HALF), :]
        owner = lax.broadcasted_iota(jnp.int32, (HALF, TILE), 0) + first
        pick_id = row_of if which == 0 else col_of
        px = peak_x[...]
        sx = sum_x[...]
        highest = peak
        for s in range(EXTRA):
            highest = jnp.maximum(highest, jnp.where(owner == pick_id(s), px[s : s + 1], LOWEST))
        total = sum_r[pl.ds(first, HALF), :] * jnp.exp2(peak - highest)
        for s in range(EXTRA):
            shortfall = jnp.minimum(px[s : s + 1] - highest, 0.0)
            total = total + jnp.where(owner == pick_id(s), sx[s : s + 1] * jnp.exp2(shortfall), 0.0)
        return highest + jnp.log2(total)

    def columns_of(pot):
        rows = pot.shape[0]
        full = jnp.concatenate([pot, jnp.zeros((TILE - rows, TILE), jnp.float32)], axis=0)
        return full.T

    def pick(cols, n):
        lane = lax.broadcasted_iota(jnp.int32, (TILE, TILE), 1)
        return jnp.sum(jnp.where(lane == n, cols, 0.0), axis=1, keepdims=True)

    def row_extras(cols):
        grouped(lambda s: keep_extra(s, *peak_and_sum(AT[FIXED + s] + pick(cols, col_of(s)))), EXTRA, 4)

    def row_half(cols, first):
        def group(g, carry):
            near = pltpu.roll(cols, lax.rem(TILE - 8 * g, TILE), 1)
            for u in range(8):
                r = 8 * g + u + first
                peak, total = peak_and_sum(AT[r] + near[:, u : u + 1])
                peak_r[pl.ds(r, 1), :] = peak
                sum_r[pl.ds(r, 1), :] = total
            return carry

        lax.fori_loop(0, HALF // 8, group, 0)

    def col_pass():
        cols = columns_of(s_pot[...])

        def group(g, carry):
            near = pltpu.roll(cols, lax.rem(TILE - 8 * g, TILE), 1)
            for u in range(8):
                c = 8 * g + u
                first = A[c] + near[:, u : u + 1]
                second = A[c + COL_TILES] + near[:, COL_TILES + u : COL_TILES + u + 1]
                peak, total = peak_and_sum(jnp.concatenate([first, second], axis=0))
                peak_r[pl.ds(c, 1), :] = peak
                sum_r[pl.ds(c, 1), :] = total
            return carry

        lax.fori_loop(0, COL_TILES // 8, group, 0)
        grouped(lambda s: keep_extra(s, *peak_and_sum(A[FIXED + s] + pick(cols, row_of(s)))), EXTRA, 4)

    def to_plane(src, dst, ssem, rsem):
        def send(d, c):
            remote(src, dst, ssem, rsem, (i, lax.rem(k + d, NT))).start()
            return c

        lax.fori_loop(1, NT, send, 0)

    def to_line(src, dst, ssem, rsem):
        def send(d, c):
            to = lax.rem(i + lax.rem(d + 6, NS - 1) + 1, NS)
            remote(src, dst, ssem, rsem, (to, k)).start()
            return c

        lax.fori_loop(0, NS - 1, send, 0)

    mine = pl.multiple_of(HALF * core, HALF)
    other = HALF - mine
    grouped(extra_first, EXTRA, 4)
    for it in range(ITERS):
        if it > 0:
            cols = columns_of(t_pot[...])
            row_extras(cols)
            row_half(cols, other)
        half_out[it] = fold(other, 0)
        remote(half_out.at[it], half_in.at[it], half_send.at[it], half_recv.at[it], (i, sibling)).start()
        if it > 0:
            row_half(cols, mine)
        one = fold(mine, 0)
        drain(half_in.at[it], half_recv.at[it])
        two = half_in[it]
        top = jnp.maximum(one, two)
        both = top + jnp.log2(jnp.exp2(one - top) + jnp.exp2(two - top))
        if it == 0:
            row_out[...] = both
            row_in[k] = both
            to_plane(row_out, row_in.at[k], row_send.at[0], row_recv.at[0])
            to_line(own_b, b_parts.at[i], mass_send.at[1], mass_recv.at[1])
            to_plane(own_a, a_parts.at[k], mass_send.at[0], mass_recv.at[0])
            grouped(extra_second, EXTRA, 4)
            grouped(fixed_second, COL_TILES, 4)
            drain(row_in.at[pl.ds(0, NT - 1)], row_recv.at[0])
            total = lse_leading(row_in[...].reshape(NS, ROW_TILES, TILE))
            drain(a_parts.at[pl.ds(0, NT - 1)], mass_recv.at[0])
            for n in range(NT):
                a_all[2 * n : 2 * n + 2, :] = a_parts[n]
        else:
            rest = (both - row_tot[pl.ds(mine, HALF), :]).astype(jnp.bfloat16)
            row_out16[it - 1] = rest
            row_in16[it - 1, k] = rest
            to_plane(row_out16.at[it - 1], row_in16.at[it - 1, k], row_send.at[it], row_recv.at[it])
            drain(row_in16.at[it - 1, pl.ds(0, NT - 1)], row_recv.at[it])
            parts = row_in16[it - 1].reshape(NS, ROW_TILES, TILE).astype(jnp.float32)
            total = row_tot[...] + lse_leading(parts)
        row_tot[...] = total
        s_pot[...] = a_all[...] - total

        col_pass()
        logs = fold(0, 1)
        if it == 0:
            col_out[...] = logs
            col_in[i] = logs
            to_line(col_out, col_in.at[i], col_send.at[0], col_recv.at[0])
            drain(b_parts.at[pl.ds(0, NS - 1)], mass_recv.at[1])
            for n in range(NS):
                b_all[2 * n : 2 * n + 2, :] = b_parts[n]
            drain(col_in.at[pl.ds(0, NS - 1)], col_recv.at[0])
            total = lse_leading(col_in[...])
        elif it + 1 < ITERS:
            rest = (logs - col_tot[...]).astype(jnp.bfloat16)
            col_out16[...] = rest
            col_in16[i] = rest
            to_line(col_out16, col_in16.at[i], col_send.at[it], col_recv.at[it])
            drain(col_in16.at[pl.ds(0, NS - 1)], col_recv.at[it])
            total = col_tot[...] + lse_leading(col_in16[...].astype(jnp.float32))
        if it + 1 < ITERS:
            col_tot[...] = total
            t_pot[...] = b_all[...] - total
    for n in range(NS):
        fin_out[n] = logs[2 * n : 2 * n + 2]
    fin_in[i] = fin_out[i]

    def send_fin(d, c):
        to = lax.rem(i + lax.rem(d + 6, NS - 1) + 1, NS)
        remote(fin_out.at[to], fin_in.at[i], col_send.at[2], col_recv.at[2], (to, k)).start()
        return c

    lax.fori_loop(0, NS - 1, send_fin, 0)
    s_out[...] = s_pot[pl.ds(2 * k, 2), :] * LN2
    drain(Y.at[pl.ds(0, 15)], z_send.at[0])
    drain(Y.at[pl.ds(0, 15)], z_send.at[1])
    drain(X.at[pl.ds(0, 30)], x_send.at[0])
    drain(X.at[pl.ds(0, 32)], x_send.at[1])
    drain(a_parts.at[pl.ds(0, NT - 1)], mass_send.at[0])
    drain(b_parts.at[pl.ds(0, NS - 1)], mass_send.at[1])
    for it in range(ITERS):
        drain(half_in.at[it], half_send.at[it])
    drain(row_in.at[pl.ds(0, NT - 1)], row_send.at[0])
    for it in range(1, ITERS):
        drain(row_in16.at[it - 1, pl.ds(0, NT - 1)], row_send.at[it])
    drain(col_in.at[pl.ds(0, NS - 1)], col_send.at[0])
    drain(col_in16.at[pl.ds(0, NS - 1)], col_send.at[1])
    drain(fin_in.at[pl.ds(0, NS - 1)], col_send.at[2])
    drain(fin_in.at[pl.ds(0, NS - 1)], col_recv.at[2])
    t_out[...] = (own_b[...] - lse_leading(fin_in[...])) * LN2


def shards(src_points, src_logmass, tgt_points, tgt_logmass, tile_list, tile_count):
    f32, bf16 = jnp.float32, jnp.bfloat16
    vmem = pl.BlockSpec(memory_space=pltpu.VMEM)
    smem = pl.BlockSpec(memory_space=pltpu.SMEM)
    hbm = pl.BlockSpec(memory_space=pltpu.HBM)
    dma = pltpu.SemaphoreType.DMA
    s, t = pl.pallas_call(
        kernel,
        out_shape=(
            jax.ShapeDtypeStruct((2, TILE), f32),
            jax.ShapeDtypeStruct((2, TILE), f32),
        ),
        in_specs=[hbm, vmem, hbm, vmem, smem, smem],
        out_specs=(vmem, vmem),
        scratch_shapes=[
            pltpu.VMEM((ROW_TILES, TILE, D), bf16),
            pltpu.VMEM((COL_TILES, TILE, D), bf16),
            pltpu.VMEM((SLOTS, TILE, TILE), f32),
            pltpu.VMEM((SLOTS, TILE, TILE), f32),
            pltpu.VMEM((NT, 2, TILE), f32),
            pltpu.VMEM((NS, 2, TILE), f32),
            pltpu.VMEM((ROW_TILES, TILE), f32),
            pltpu.VMEM((COL_TILES, TILE), f32),
            pltpu.VMEM((2, TILE), f32),
            pltpu.VMEM((2, TILE), f32),
            pltpu.VMEM((ROW_TILES, TILE), f32),
            pltpu.VMEM((ROW_TILES, TILE), f32),
            pltpu.VMEM((EXTRA, TILE), f32),
            pltpu.VMEM((EXTRA, TILE), f32),
            pltpu.VMEM((ROW_TILES, TILE), f32),
            pltpu.VMEM((COL_TILES, TILE), f32),
            pltpu.VMEM((ROW_TILES, TILE), f32),
            pltpu.VMEM((COL_TILES, TILE), f32),
            pltpu.VMEM((ITERS, HALF, TILE), f32),
            pltpu.VMEM((ITERS, HALF, TILE), f32),
            pltpu.VMEM((HALF, TILE), f32),
            pltpu.VMEM((NT, HALF, TILE), f32),
            pltpu.VMEM((ITERS - 1, HALF, TILE), bf16),
            pltpu.VMEM((ITERS - 1, NT, HALF, TILE), bf16),
            pltpu.VMEM((COL_TILES, TILE), f32),
            pltpu.VMEM((NS, COL_TILES, TILE), f32),
            pltpu.VMEM((COL_TILES, TILE), bf16),
            pltpu.VMEM((NS, COL_TILES, TILE), bf16),
            pltpu.VMEM((NS, 2, TILE), f32),
            pltpu.VMEM((NS, 2, TILE), f32),
            dma((32,)),
            dma((32,)),
            dma((2,)),
            dma((4,)),
            dma((16,)),
            dma((2,)),
            dma((1,)),
            dma((2,)),
            dma((2,)),
            dma((2,)),
            dma((ITERS,)),
            dma((ITERS,)),
            dma((ITERS,)),
            dma((ITERS,)),
            dma((ITERS,)),
            dma((ITERS,)),
        ],
        compiler_params=pltpu.CompilerParams(
            collective_id=0, has_side_effects=True, vmem_limit_bytes=60 * 2**20
        ),
    )(
        src_points.reshape(2, TILE, D),
        src_logmass,
        tgt_points.reshape(2, TILE, D),
        tgt_logmass,
        tile_list.reshape(SLOTS, 2).T,
        tile_count,
    )
    return s.reshape(1, 2 * TILE), t.reshape(1, 2 * TILE)


def solution(mesh):
    placed = (
        P("src", "tgt", None),
        P("src", "tgt"),
        P("tgt", "src", None),
        P("tgt", "src"),
        P("src", "tgt", None, None),
        P("src", "tgt"),
    )
    return jax.shard_map(
        shards,
        mesh=mesh,
        in_specs=placed,
        out_specs=(P("src", "tgt"), P("tgt", "src")),
        check_vma=False,
    )
```

```python
import math

import jax
import jax.numpy as jnp
from jax import lax
from jax.experimental import pallas as pl
from jax.experimental.pallas import tpu as pltpu
from jax.sharding import PartitionSpec as P

MESH = pl.DeviceIdType.MESH
TILE = 128
D = 256
ROW_TILES = 64
COL_TILES = 32
SLOTS = 80
FIXED = 64
EXTRA = SLOTS - FIXED
ITERS = 3
NS = 16
NT = 32
PIECES = 4
PLANE = sorted(
    ((x, y, c) for x in range(4) for y in range(4) for c in range(2) if x + y + c),
    key=lambda d: -(d[0] % 4 * (4 - d[0]) + d[1] % 4 * (4 - d[1])),
)
PIECE = 2 * TILE // PIECES
QUARTER = COL_TILES // 2
HALF = ROW_TILES // 2
LOG2E = math.log2(math.e)
LN2 = math.log(2.0)
SCALE = -20.0 * LOG2E
LOWEST = -1.0e30
NT_DIMS = (((1,), (1,)), ((), ()))


def scaled_cost(left, right):
    products = lax.dot_general(left, right, NT_DIMS, preferred_element_type=jnp.float32)
    return (1.0 - products).astype(jnp.bfloat16).astype(jnp.float32) * SCALE


def peak_and_sum(scores):
    peak = jnp.max(scores, axis=0, keepdims=True)
    return peak, jnp.sum(jnp.exp2(scores - peak), axis=0, keepdims=True)


def lse_leading(parts):
    peak = jnp.max(parts, axis=0)
    return peak + jnp.log2(jnp.sum(jnp.exp2(parts - peak[None]), axis=0))


def kernel(
    xp, am, yp, bm, tiles_hbm, count_hbm, pots,
    tiles, count,
    X, Y, A, AT, a_parts, b_parts, a_all, b_all, own_a, own_b,
    peak_r, sum_r, peak_x, sum_x, s_pot, t_pot, row_tot, col_tot,
    half_out, half_in, row_out, row_in, row_out16, row_in16,
    spread, pair_out, pair_in, col_out, col_in, col_out16, col_in16, fin_out, fin_in,
    z_up, z_dn, z_send, xa, xb, x_send, sib_recv, mass_recv, mass_send, local,
    half_recv, half_send, row_recv, row_send, col_recv, col_send, pair_sem,
):
    i = lax.axis_index("src")
    k = lax.axis_index("tgt")
    core = lax.rem(k, 2)
    sibling = k + 1 - 2 * core
    up = lax.rem(i + 1, NS)
    dn = lax.rem(i + NS - 1, NS)
    odd = lax.rem(i, 2)
    partner = i + 1 - 2 * odd
    px, py = k // 8, lax.rem(k // 2, 4)
    pa = px * (1 - core) + py * core
    pb = py * (1 - core) + px * core

    def at(da, db):
        a, b = lax.rem(pa + 4 + da, 4), lax.rem(pb + 4 + db, 4)
        return (a * (1 - core) + b * core) * 8 + (b * (1 - core) + a * core) * 2 + core

    barrier = pltpu.get_barrier_semaphore()
    near = ((up, k), (dn, k), (i, at(1, 0)), (i, at(-1, 0)), (i, at(0, 1)), (i, at(0, -1)), (i, sibling))
    for dev in near:
        pl.semaphore_signal(barrier, inc=1, device_id=dev, device_id_type=MESH)
    own_x = pltpu.make_async_copy(xp, X.at[pl.ds(2 * k, 2)], local.at[0])
    own_y = pltpu.make_async_copy(yp, Y.at[pl.ds(2 * i, 2)], local.at[1])
    own_tiles = pltpu.make_async_copy(tiles_hbm, tiles, local.at[2])
    own_count = pltpu.make_async_copy(count_hbm, count, local.at[3])
    for copy in (own_y, own_x, own_tiles, own_count):
        copy.start()
    own_x.wait()
    own_y.wait()
    pl.semaphore_wait(barrier, len(near))

    def remote(src, dst, ssem, rsem, dev):
        return pltpu.make_async_remote_copy(
            src_ref=src, dst_ref=dst, send_sem=ssem, recv_sem=rsem, device_id=dev, device_id_type=MESH
        )

    def drain(like, sem):
        pltpu.make_async_copy(like, like, sem).wait()

    def to_plane(src, dst, ssem, rsem):
        for dx, dy, dc in PLANE:
            to = lax.rem(px + dx, 4) * 8 + lax.rem(py + dy, 4) * 2 + lax.rem(core + dc, 2)
            remote(src, dst, ssem, rsem, (i, to)).start()

    def z_piece(shard, q):
        return Y.at[2 * shard + q // (PIECES // 2), pl.ds((q % (PIECES // 2)) * PIECE, PIECE)]

    def z_copy(shard, q, distance, direction, to):
        block = z_piece(shard, q)
        sem = (z_up, z_dn)[direction].at[(distance - 1) * PIECES + q]
        return remote(block, block, z_send.at[direction], sem, (to, k))

    def z_wait(shard, q, distance, direction):
        drain(z_piece(shard, q), (z_up, z_dn)[direction].at[(distance - 1) * PIECES + q])

    def x_block(da, db):
        return X.at[pl.ds(2 * at(da, db), 2)]

    def x_tile(da, db, t):
        return X.at[2 * at(da, db) + t]

    def x_copy(block, sem, da, db):
        remote(block, block, x_send.at[0], sem, (i, at(da, db))).start()

    def x_sibling(da, db):
        block = x_block(da, db)
        remote(block, block, x_send.at[1], sib_recv.at[0], (i, sibling)).start()

    OFFSETS = (0, -1, 1, 2)

    def x_both(j):
        block = x_block(OFFSETS[j], 0)
        x_copy(block, xb.at[j], 0, 1)
        x_copy(block, xb.at[4 + j], 0, -1)
        x_sibling(OFFSETS[j], 0)

    def x_step(step):
        if step == 1:
            for j, da, tile in ((1, -1, 0), (2, 1, 1)):
                drain(x_block(da, 0), xa.at[j - 1])
                x_copy(x_tile(da, 0, tile), xa.at[1 + j], -da, 0)
                x_both(j)
        if step == 2:
            drain(x_tile(2, 0, 0), xa.at[2])
            drain(x_tile(2, 0, 1), xa.at[3])
            x_both(3)
        for j in {2: (0,), 3: (1, 2), 4: (3,)}.get(step, ()):
            for n, db in ((0, -1), (1, 1)):
                drain(x_block(OFFSETS[j], db), xb.at[4 * n + j])
                x_copy(x_tile(OFFSETS[j], db, n), xb.at[8 + 4 * n + j], 0, -db)
                x_sibling(OFFSETS[j], db)
        for j in {4: (0,), 5: (1, 2, 3)}.get(step, ()):
            for n in range(2):
                drain(x_tile(OFFSETS[j], 2, n), xb.at[8 + 4 * n + j])
            x_sibling(OFFSETS[j], 2)
        if step == 6:
            drain(X.at[pl.ds(0, 2 * NS)], sib_recv.at[0])

    def fixed_first(c):
        pair = jnp.concatenate([X[c], X[c + COL_TILES]], axis=0)
        costs = scaled_cost(Y[c], pair)
        peak, total = peak_and_sum(costs)
        for h in range(2):
            r = c + COL_TILES * h
            AT[r] = costs[:, TILE * h : TILE * (h + 1)]
            peak_r[pl.ds(r, 1), :] = peak[:, TILE * h : TILE * (h + 1)]
            sum_r[pl.ds(r, 1), :] = total[:, TILE * h : TILE * (h + 1)]

    def fixed_second(c):
        for h in range(2):
            r = c + COL_TILES * h
            A[r] = scaled_cost(X[r], Y[c])

    def shards_from(low, high, *bodies):
        def shard(n, carry):
            for half in range(2):
                for body in bodies:
                    body(2 * lax.rem(i + n, NS) + half)
            return carry

        lax.fori_loop(NS + low, NS + high, shard, 0)

    for q in range(PIECES):
        for direction, to in ((0, up), (1, dn)):
            z_copy(i, q, 1, direction, to).start()
    x_copy(x_block(0, 0), xa.at[0], 1, 0)
    x_copy(x_block(0, 0), xa.at[1], -1, 0)
    x_both(0)
    own_tiles.wait()
    own_count.wait()
    spread[...] = jnp.zeros((TILE, TILE), jnp.float32)
    own_a[0:1, :] = am[:, 0:TILE].astype(jnp.float32) * LOG2E
    own_a[1:2, :] = am[:, TILE:].astype(jnp.float32) * LOG2E
    own_b[0:1, :] = bm[:, 0:TILE].astype(jnp.float32) * LOG2E
    own_b[1:2, :] = bm[:, TILE:].astype(jnp.float32) * LOG2E
    a_parts[k] = own_a[...]
    b_parts[i] = own_b[...]
    for step in range(1, 8):
        for q in range(PIECES):
            for direction, shard, to in ((0, lax.rem(i + NS - step, NS), up), (1, lax.rem(i + step, NS), dn)):
                z_wait(shard, q, step, direction)
                if step < 7 or q // (PIECES // 2) == direction:
                    z_copy(shard, q, step + 1, direction, to).start()
        x_step(step)
        if step == 6:
            to_plane(own_a, a_parts.at[k], mass_send.at[0], mass_recv.at[0])
            shards_from(-2, 3, fixed_first, fixed_second)
        if step == 7:
            shards_from(-6, -2, fixed_first)
            shards_from(3, 7, fixed_first)
    far = lax.rem(i + 8, NS)
    for q in range(PIECES):
        z_wait(far, q, 8, q // (PIECES // 2))
    shards_from(7, 10, fixed_first)
    live_count = count[0, 0]

    def alive(s):
        return jnp.full((1, TILE), live_count, jnp.int32) > FIXED + s

    def keep_extra(s, peak, total):
        peak_x[pl.ds(s, 1), :] = jnp.where(alive(s), peak, LOWEST)
        sum_x[pl.ds(s, 1), :] = total

    def row_of(s):
        return tiles[0, FIXED + s]

    def col_of(s):
        return tiles[1, FIXED + s]

    def grouped(body, count, size):
        def group(g, carry):
            for u in range(size):
                body(size * g + u)
            return carry

        lax.fori_loop(0, count // size, group, 0)

    def extra_first(s):
        costs = scaled_cost(Y[col_of(s)], X[row_of(s)])
        AT[FIXED + s] = costs
        keep_extra(s, *peak_and_sum(costs))

    def extra_second(s):
        A[FIXED + s] = scaled_cost(X[row_of(s)], Y[col_of(s)])

    def fold(first, size, which):
        peak = peak_r[pl.ds(first, size), :]
        owner = lax.broadcasted_iota(jnp.int32, (size, TILE), 0) + first
        pick_id = row_of if which == 0 else col_of
        px = peak_x[...]
        sx = sum_x[...]
        highest = peak
        for s in range(EXTRA):
            highest = jnp.maximum(highest, jnp.where(owner == pick_id(s), px[s : s + 1], LOWEST))
        total = sum_r[pl.ds(first, size), :] * jnp.exp2(peak - highest)
        for s in range(EXTRA):
            shortfall = jnp.minimum(px[s : s + 1] - highest, 0.0)
            total = total + jnp.where(owner == pick_id(s), sx[s : s + 1] * jnp.exp2(shortfall), 0.0)
        return highest + jnp.log2(total)

    def columns_of(pot, first, which):
        spread[0:first, :] = pot[...]
        for s in range(EXTRA):
            spread[first + s : first + s + 1, :] = pot[pl.ds(row_of(s) if which == 0 else col_of(s), 1), :]
        return spread[...].T

    def lanes_from(cols, first):
        return pltpu.roll(cols, lax.rem(TILE - first, TILE), 1)

    def extras(cols, costs, first):
        for g in range(EXTRA // 8):
            for u in range(8):
                s = 8 * g + u
                keep_extra(s, *peak_and_sum(costs[FIXED + s] + cols[:, first + s : first + s + 1]))

    def row_half(cols, first):
        def group(g, carry):
            near = lanes_from(cols, 8 * g)
            for u in range(8):
                r = 8 * g + u + first
                peak, total = peak_and_sum(AT[r] + near[:, u : u + 1])
                peak_r[pl.ds(r, 1), :] = peak
                sum_r[pl.ds(r, 1), :] = total
            return carry

        lax.fori_loop(0, HALF // 8, group, 0)

    def col_half(cols, first):
        def group(g, carry):
            near = lanes_from(cols, 8 * g + first)
            for u in range(8):
                c = 8 * g + u + first
                one = A[c] + near[:, u : u + 1]
                two = A[c + COL_TILES] + near[:, COL_TILES + u : COL_TILES + u + 1]
                peak = jnp.max(jnp.maximum(one, two), axis=0, keepdims=True)
                total = jnp.sum(jnp.exp2(one - peak) + jnp.exp2(two - peak), axis=0, keepdims=True)
                peak_r[pl.ds(c, 1), :] = peak
                sum_r[pl.ds(c, 1), :] = total
            return carry

        lax.fori_loop(0, COL_TILES // 16, group, 0)

    def to_line(src, dst, ssem, rsem):
        def send(d, c):
            to = lax.rem(i + lax.rem(d + 6, NS - 1) + 1, NS)
            remote(src, dst, ssem, rsem, (to, k)).start()
            return c

        lax.fori_loop(0, NS - 1, send, 0)

    mine = pl.multiple_of(HALF * core, HALF)
    other = HALF - mine
    mine_z = pl.multiple_of(QUARTER * odd, QUARTER)
    other_z = QUARTER - mine_z
    grouped(extra_first, EXTRA, 4)
    for it in range(ITERS):
        if it > 0:
            cols = columns_of(t_pot, COL_TILES, 1)
            extras(cols, AT, COL_TILES)
            row_half(cols, other)
        half_out[it] = fold(other, HALF, 0)
        remote(half_out.at[it], half_in.at[it], half_send.at[it], half_recv.at[it], (i, sibling)).start()
        if it > 0:
            row_half(cols, mine)
        one = fold(mine, HALF, 0)
        drain(half_in.at[it], half_recv.at[it])
        two = half_in[it]
        top = jnp.maximum(one, two)
        both = top + jnp.log2(jnp.exp2(one - top) + jnp.exp2(two - top))
        if it == 0:
            row_out[...] = both
            row_in[k] = both
            to_plane(row_out, row_in.at[k], row_send.at[0], row_recv.at[0])
            to_line(own_b, b_parts.at[i], mass_send.at[1], mass_recv.at[1])
            grouped(extra_second, EXTRA, 4)
            shards_from(3, 14, fixed_second)
            drain(row_in.at[pl.ds(0, NT - 1)], row_recv.at[0])
            total = lse_leading(row_in[...].reshape(NS, ROW_TILES, TILE))
            drain(a_parts.at[pl.ds(0, NT - 1)], mass_recv.at[0])
            for n in range(NT):
                a_all[2 * n : 2 * n + 2, :] = a_parts[n]
        else:
            rest = (both - row_tot[pl.ds(mine, HALF), :]).astype(jnp.bfloat16)
            row_out16[it - 1] = rest
            row_in16[it - 1, k] = rest
            to_plane(row_out16.at[it - 1], row_in16.at[it - 1, k], row_send.at[it], row_recv.at[it])
            drain(row_in16.at[it - 1, pl.ds(0, NT - 1)], row_recv.at[it])
            parts = row_in16[it - 1].reshape(NS, ROW_TILES, TILE).astype(jnp.float32)
            total = row_tot[...] + lse_leading(parts)
        row_tot[...] = total
        s_pot[...] = a_all[...] - total

        cols = columns_of(s_pot, ROW_TILES, 0)
        extras(cols, A, ROW_TILES)
        if it == 0:
            col_half(cols, other_z)
            pair_out[...] = fold(other_z, QUARTER, 1)
            remote(pair_out, pair_in, pair_sem.at[0], pair_sem.at[1], (partner, k)).start()
            col_half(cols, mine_z)
            one = fold(mine_z, QUARTER, 1)
            drain(b_parts.at[pl.ds(0, NS - 1)], mass_recv.at[1])
            for n in range(NS):
                b_all[2 * n : 2 * n + 2, :] = b_parts[n]
            drain(pair_in, pair_sem.at[1])
            two = pair_in[...]
            top = jnp.maximum(one, two)
            both = top + jnp.log2(jnp.exp2(one - top) + jnp.exp2(two - top))
            col_out[...] = both
            col_in[i] = both
            to_line(col_out, col_in.at[i], col_send.at[0], col_recv.at[0])
            drain(col_in.at[pl.ds(0, NS - 1)], col_recv.at[0])
            total = lse_leading(col_in[...].reshape(NS // 2, COL_TILES, TILE))
        else:
            col_half(cols, 0)
            col_half(cols, QUARTER)
            logs = fold(0, COL_TILES, 1)
        if 0 < it < ITERS - 1:
            rest = (logs - col_tot[...]).astype(jnp.bfloat16)
            col_out16[...] = rest
            col_in16[i] = rest
            to_line(col_out16, col_in16.at[i], col_send.at[it], col_recv.at[it])
            drain(col_in16.at[pl.ds(0, NS - 1)], col_recv.at[it])
            total = col_tot[...] + lse_leading(col_in16[...].astype(jnp.float32))
        if it + 1 < ITERS:
            col_tot[...] = total
            t_pot[...] = b_all[...] - total
    for n in range(NS):
        fin_out[n] = logs[2 * n : 2 * n + 2]
    fin_in[i] = fin_out[i]

    def send_fin(d, c):
        to = lax.rem(i + lax.rem(d + 6, NS - 1) + 1, NS)
        remote(fin_out.at[to], fin_in.at[i], col_send.at[2], col_recv.at[2], (to, k)).start()
        return c

    lax.fori_loop(0, NS - 1, send_fin, 0)
    pots[0] = s_pot[pl.ds(2 * k, 2), :] * LN2
    drain(Y.at[pl.ds(0, 15)], z_send.at[0])
    drain(Y.at[pl.ds(0, 15)], z_send.at[1])
    drain(X.at[pl.ds(0, 30)], x_send.at[0])
    drain(X.at[pl.ds(0, 32)], x_send.at[1])
    drain(a_parts.at[pl.ds(0, NT - 1)], mass_send.at[0])
    drain(b_parts.at[pl.ds(0, NS - 1)], mass_send.at[1])
    for it in range(ITERS):
        drain(half_in.at[it], half_send.at[it])
    drain(row_in.at[pl.ds(0, NT - 1)], row_send.at[0])
    for it in range(1, ITERS):
        drain(row_in16.at[it - 1, pl.ds(0, NT - 1)], row_send.at[it])
    drain(pair_in, pair_sem.at[0])
    drain(col_in.at[pl.ds(0, NS - 1)], col_send.at[0])
    drain(col_in16.at[pl.ds(0, NS - 1)], col_send.at[1])
    drain(fin_in.at[pl.ds(0, NS - 1)], col_send.at[2])
    drain(fin_in.at[pl.ds(0, NS - 1)], col_recv.at[2])
    pots[1] = (own_b[...] - lse_leading(fin_in[...])) * LN2


def shards(src_points, src_logmass, tgt_points, tgt_logmass, tile_list, tile_count):
    f32, bf16 = jnp.float32, jnp.bfloat16
    vmem = pl.BlockSpec(memory_space=pltpu.VMEM)
    hbm = pl.BlockSpec(memory_space=pltpu.HBM)
    dma = pltpu.SemaphoreType.DMA
    pots = pl.pallas_call(
        kernel,
        out_shape=jax.ShapeDtypeStruct((2, 2, TILE), f32),
        in_specs=[hbm, vmem, hbm, vmem, hbm, hbm],
        out_specs=vmem,
        scratch_shapes=[
            pltpu.SMEM((2, SLOTS), jnp.int32),
            pltpu.SMEM((1, 1), jnp.int32),
            pltpu.VMEM((ROW_TILES, TILE, D), bf16),
            pltpu.VMEM((COL_TILES, TILE, D), bf16),
            pltpu.VMEM((SLOTS, TILE, TILE), f32),
            pltpu.VMEM((SLOTS, TILE, TILE), f32),
            pltpu.VMEM((NT, 2, TILE), f32),
            pltpu.VMEM((NS, 2, TILE), f32),
            pltpu.VMEM((ROW_TILES, TILE), f32),
            pltpu.VMEM((COL_TILES, TILE), f32),
            pltpu.VMEM((2, TILE), f32),
            pltpu.VMEM((2, TILE), f32),
            pltpu.VMEM((ROW_TILES, TILE), f32),
            pltpu.VMEM((ROW_TILES, TILE), f32),
            pltpu.VMEM((EXTRA, TILE), f32),
            pltpu.VMEM((EXTRA, TILE), f32),
            pltpu.VMEM((ROW_TILES, TILE), f32),
            pltpu.VMEM((COL_TILES, TILE), f32),
            pltpu.VMEM((ROW_TILES, TILE), f32),
            pltpu.VMEM((COL_TILES, TILE), f32),
            pltpu.VMEM((ITERS, HALF, TILE), f32),
            pltpu.VMEM((ITERS, HALF, TILE), f32),
            pltpu.VMEM((HALF, TILE), f32),
            pltpu.VMEM((NT, HALF, TILE), f32),
            pltpu.VMEM((ITERS - 1, HALF, TILE), bf16),
            pltpu.VMEM((ITERS - 1, NT, HALF, TILE), bf16),
            pltpu.VMEM((TILE, TILE), f32),
            pltpu.VMEM((QUARTER, TILE), f32),
            pltpu.VMEM((QUARTER, TILE), f32),
            pltpu.VMEM((QUARTER, TILE), f32),
            pltpu.VMEM((NS, QUARTER, TILE), f32),
            pltpu.VMEM((COL_TILES, TILE), bf16),
            pltpu.VMEM((NS, COL_TILES, TILE), bf16),
            pltpu.VMEM((NS, 2, TILE), f32),
            pltpu.VMEM((NS, 2, TILE), f32),
            dma((8 * PIECES,)),
            dma((8 * PIECES,)),
            dma((2,)),
            dma((4,)),
            dma((16,)),
            dma((2,)),
            dma((1,)),
            dma((2,)),
            dma((2,)),
            dma((4,)),
            dma((ITERS,)),
            dma((ITERS,)),
            dma((ITERS,)),
            dma((ITERS,)),
            dma((ITERS,)),
            dma((ITERS,)),
            dma((2,)),
        ],
        compiler_params=pltpu.CompilerParams(
            collective_id=0, has_side_effects=True, vmem_limit_bytes=60 * 2**20
        ),
    )(
        src_points.reshape(2, TILE, D),
        src_logmass,
        tgt_points.reshape(2, TILE, D),
        tgt_logmass,
        tile_list.reshape(SLOTS, 2).T,
        tile_count,
    )
    return pots[0].reshape(1, 2 * TILE), pots[1].reshape(1, 2 * TILE)


def solution(mesh):
    placed = (
        P("src", "tgt", None),
        P("src", "tgt"),
        P("tgt", "src", None),
        P("tgt", "src"),
        P("src", "tgt", None, None),
        P("src", "tgt"),
    )
    return jax.shard_map(
        shards,
        mesh=mesh,
        in_specs=placed,
        out_specs=(P("src", "tgt"), P("tgt", "src")),
        check_vma=False,
    )
```

```python
import math

import jax
import jax.numpy as jnp
from jax import lax
from jax.experimental import pallas as pl
from jax.experimental.pallas import tpu as pltpu
from jax.sharding import PartitionSpec as P

MESH = pl.DeviceIdType.MESH
TILE = 128
D = 256
ROW_TILES = 64
COL_TILES = 32
SLOTS = 80
FIXED = 64
EXTRA = SLOTS - FIXED
ITERS = 3
NS = 16
NT = 32
PIECES = 4
PLANE = sorted(
    ((x, y, c) for x in range(4) for y in range(4) for c in range(2) if x + y + c),
    key=lambda d: -(d[0] % 4 * (4 - d[0]) + d[1] % 4 * (4 - d[1])),
)
PIECE = 2 * TILE // PIECES
QUARTER = COL_TILES // 2
HALF = ROW_TILES // 2
LOG2E = math.log2(math.e)
LN2 = math.log(2.0)
SCALE = -20.0 * LOG2E
LOWEST = -1.0e30
NT_DIMS = (((1,), (1,)), ((), ()))


def scaled_cost(left, right):
    products = lax.dot_general(left, right, NT_DIMS, preferred_element_type=jnp.float32)
    return (1.0 - products).astype(jnp.bfloat16).astype(jnp.float32) * SCALE


def peak_and_sum(scores):
    peak = jnp.max(scores, axis=0, keepdims=True)
    return peak, jnp.sum(jnp.exp2(scores - peak), axis=0, keepdims=True)


def lse_leading(parts):
    peak = jnp.max(parts, axis=0)
    return peak + jnp.log2(jnp.sum(jnp.exp2(parts - peak[None]), axis=0))


def kernel(
    xp, am, yp, bm, tiles_hbm, count_hbm, pots,
    tiles, count,
    X, Y, A, AT, a_parts, b_parts, a_all, b_all, own_a, own_b,
    peak_r, sum_r, peak_x, sum_x, s_pot, t_pot, row_tot, col_tot,
    half_out, half_in, row_out, row_in, row_out16, row_in16,
    spread, pair_out, pair_in, col_out, col_in, col_out16, col_in16, fin_out, fin_in,
    z_up, z_dn, z_send, xa, xb, x_send, sib_recv, mass_recv, mass_send, local,
    half_recv, half_send, row_recv, row_send, col_recv, col_send, pair_sem,
):
    i = lax.axis_index("src")
    k = lax.axis_index("tgt")
    core = lax.rem(k, 2)
    sibling = k + 1 - 2 * core
    up = lax.rem(i + 1, NS)
    dn = lax.rem(i + NS - 1, NS)
    odd = lax.rem(i, 2)
    partner = i + 1 - 2 * odd
    px, py = k // 8, lax.rem(k // 2, 4)
    pa = px * (1 - core) + py * core
    pb = py * (1 - core) + px * core

    def at(da, db):
        a, b = lax.rem(pa + 4 + da, 4), lax.rem(pb + 4 + db, 4)
        return (a * (1 - core) + b * core) * 8 + (b * (1 - core) + a * core) * 2 + core

    barrier = pltpu.get_barrier_semaphore()
    near = ((up, k), (dn, k), (i, at(1, 0)), (i, at(-1, 0)), (i, at(0, 1)), (i, at(0, -1)), (i, sibling))
    for dev in near:
        pl.semaphore_signal(barrier, inc=1, device_id=dev, device_id_type=MESH)
    own_x = pltpu.make_async_copy(xp, X.at[pl.ds(2 * k, 2)], local.at[0])
    own_y = pltpu.make_async_copy(yp, Y.at[pl.ds(2 * i, 2)], local.at[1])
    own_tiles = pltpu.make_async_copy(tiles_hbm, tiles, local.at[2])
    own_count = pltpu.make_async_copy(count_hbm, count, local.at[3])
    for copy in (own_y, own_x, own_tiles, own_count):
        copy.start()
    own_x.wait()
    own_y.wait()
    pl.semaphore_wait(barrier, len(near))

    def remote(src, dst, ssem, rsem, dev):
        return pltpu.make_async_remote_copy(
            src_ref=src, dst_ref=dst, send_sem=ssem, recv_sem=rsem, device_id=dev, device_id_type=MESH
        )

    def drain(like, sem):
        pltpu.make_async_copy(like, like, sem).wait()

    def to_plane(src, dst, ssem, rsem):
        for dx, dy, dc in PLANE:
            to = lax.rem(px + dx, 4) * 8 + lax.rem(py + dy, 4) * 2 + lax.rem(core + dc, 2)
            remote(src, dst, ssem, rsem, (i, to)).start()

    def z_piece(shard, q):
        return Y.at[2 * shard + q // (PIECES // 2), pl.ds((q % (PIECES // 2)) * PIECE, PIECE)]

    def z_copy(shard, q, distance, direction, to):
        block = z_piece(shard, q)
        sem = (z_up, z_dn)[direction].at[(distance - 1) * PIECES + q]
        return remote(block, block, z_send.at[direction], sem, (to, k))

    def z_wait(shard, q, distance, direction):
        drain(z_piece(shard, q), (z_up, z_dn)[direction].at[(distance - 1) * PIECES + q])

    def x_block(da, db):
        return X.at[pl.ds(2 * at(da, db), 2)]

    def x_tile(da, db, t):
        return X.at[2 * at(da, db) + t]

    def x_copy(block, sem, da, db):
        remote(block, block, x_send.at[0], sem, (i, at(da, db))).start()

    def x_sibling(da, db):
        block = x_block(da, db)
        remote(block, block, x_send.at[1], sib_recv.at[0], (i, sibling)).start()

    OFFSETS = (0, -1, 1, 2)

    def x_both(j):
        block = x_block(OFFSETS[j], 0)
        x_copy(block, xb.at[j], 0, 1)
        x_copy(block, xb.at[4 + j], 0, -1)
        x_sibling(OFFSETS[j], 0)

    def x_step(step):
        if step == 1:
            for j, da, tile in ((1, -1, 0), (2, 1, 1)):
                drain(x_block(da, 0), xa.at[j - 1])
                x_copy(x_tile(da, 0, tile), xa.at[1 + j], -da, 0)
                x_both(j)
        if step == 2:
            drain(x_tile(2, 0, 0), xa.at[2])
            drain(x_tile(2, 0, 1), xa.at[3])
            x_both(3)
        for j in {2: (0,), 3: (1, 2), 4: (3,)}.get(step, ()):
            for n, db in ((0, -1), (1, 1)):
                drain(x_block(OFFSETS[j], db), xb.at[4 * n + j])
                x_copy(x_tile(OFFSETS[j], db, n), xb.at[8 + 4 * n + j], 0, -db)
                x_sibling(OFFSETS[j], db)
        for j in {4: (0,), 5: (1, 2, 3)}.get(step, ()):
            for n in range(2):
                drain(x_tile(OFFSETS[j], 2, n), xb.at[8 + 4 * n + j])
            x_sibling(OFFSETS[j], 2)
        if step == 6:
            drain(X.at[pl.ds(0, 2 * NS)], sib_recv.at[0])

    def fixed_first(c):
        pair = jnp.concatenate([X[c], X[c + COL_TILES]], axis=0)
        costs = scaled_cost(Y[c], pair)
        peak, total = peak_and_sum(costs)
        for h in range(2):
            r = c + COL_TILES * h
            AT[r] = costs[:, TILE * h : TILE * (h + 1)]
            peak_r[pl.ds(r, 1), :] = peak[:, TILE * h : TILE * (h + 1)]
            sum_r[pl.ds(r, 1), :] = total[:, TILE * h : TILE * (h + 1)]

    def fixed_second(c):
        for h in range(2):
            r = c + COL_TILES * h
            A[r] = scaled_cost(X[r], Y[c])

    def shards_from(low, high, *bodies):
        def shard(n, carry):
            for half in range(2):
                for body in bodies:
                    body(2 * lax.rem(i + n, NS) + half)
            return carry

        lax.fori_loop(NS + low, NS + high, shard, 0)

    for q in range(PIECES):
        for direction, to in ((0, up), (1, dn)):
            z_copy(i, q, 1, direction, to).start()
    x_copy(x_block(0, 0), xa.at[0], 1, 0)
    x_copy(x_block(0, 0), xa.at[1], -1, 0)
    x_both(0)
    own_tiles.wait()
    own_count.wait()
    spread[...] = jnp.zeros((TILE, TILE), jnp.float32)
    own_a[0:1, :] = am[:, 0:TILE].astype(jnp.float32) * LOG2E
    own_a[1:2, :] = am[:, TILE:].astype(jnp.float32) * LOG2E
    own_b[0:1, :] = bm[:, 0:TILE].astype(jnp.float32) * LOG2E
    own_b[1:2, :] = bm[:, TILE:].astype(jnp.float32) * LOG2E
    a_parts[k] = own_a[...]
    b_parts[i] = own_b[...]
    for step in range(1, 8):
        for q in range(PIECES):
            for direction, shard, to in ((0, lax.rem(i + NS - step, NS), up), (1, lax.rem(i + step, NS), dn)):
                z_wait(shard, q, step, direction)
                if step < 7 or q // (PIECES // 2) == direction:
                    z_copy(shard, q, step + 1, direction, to).start()
        x_step(step)
        if step == 6:
            to_plane(own_a, a_parts.at[k], mass_send.at[0], mass_recv.at[0])
            shards_from(-2, 3, fixed_first, fixed_second)
        if step == 7:
            shards_from(-6, -2, fixed_first)
            shards_from(3, 7, fixed_first)
    far = lax.rem(i + 8, NS)
    for q in range(PIECES):
        z_wait(far, q, 8, q // (PIECES // 2))
    shards_from(7, 10, fixed_first)
    live_count = count[0, 0]

    def alive(s):
        return jnp.full((1, TILE), live_count, jnp.int32) > FIXED + s

    def keep_extra(s, peak, total):
        peak_x[pl.ds(s, 1), :] = jnp.where(alive(s), peak, LOWEST)
        sum_x[pl.ds(s, 1), :] = total

    def row_of(s):
        return tiles[0, FIXED + s]

    def col_of(s):
        return tiles[1, FIXED + s]

    def grouped(body, count, size):
        def group(g, carry):
            for u in range(size):
                body(size * g + u)
            return carry

        lax.fori_loop(0, count // size, group, 0)

    def extra_first(s):
        costs = scaled_cost(Y[col_of(s)], X[row_of(s)])
        AT[FIXED + s] = costs
        keep_extra(s, *peak_and_sum(costs))

    def extra_second(s):
        A[FIXED + s] = scaled_cost(X[row_of(s)], Y[col_of(s)])

    def fold(first, size, which):
        peak = peak_r[pl.ds(first, size), :]
        owner = lax.broadcasted_iota(jnp.int32, (size, TILE), 0) + first
        pick_id = row_of if which == 0 else col_of
        px = peak_x[...]
        sx = sum_x[...]
        highest = peak
        for s in range(EXTRA):
            highest = jnp.maximum(highest, jnp.where(owner == pick_id(s), px[s : s + 1], LOWEST))
        total = sum_r[pl.ds(first, size), :] * jnp.exp2(peak - highest)
        for s in range(EXTRA):
            shortfall = jnp.minimum(px[s : s + 1] - highest, 0.0)
            total = total + jnp.where(owner == pick_id(s), sx[s : s + 1] * jnp.exp2(shortfall), 0.0)
        return highest + jnp.log2(total)

    def columns_of(pot, first, which):
        spread[0:first, :] = pot[...]
        for s in range(EXTRA):
            spread[first + s : first + s + 1, :] = pot[pl.ds(row_of(s) if which == 0 else col_of(s), 1), :]
        return spread[...].T

    def lanes_from(cols, first):
        return cols if isinstance(first, int) else pltpu.roll(cols, lax.rem(TILE - first, TILE), 1)

    def extras(cols, costs, first):
        for g in range(EXTRA // 8):
            for u in range(8):
                s = 8 * g + u
                keep_extra(s, *peak_and_sum(costs[FIXED + s] + cols[:, first + s : first + s + 1]))

    def row_half(cols, first):
        for c in range(HALF):
            peak, total = peak_and_sum(AT[c + first] + cols[:, c : c + 1])
            peak_r[pl.ds(c + first, 1), :] = peak
            sum_r[pl.ds(c + first, 1), :] = total

    def col_range(cols, first, size):
        near = lanes_from(cols, first)
        for u in range(size):
            c = u + first
            one = A[c] + near[:, u : u + 1]
            two = A[c + COL_TILES] + near[:, COL_TILES + u : COL_TILES + u + 1]
            peak = jnp.max(jnp.maximum(one, two), axis=0, keepdims=True)
            total = jnp.sum(jnp.exp2(one - peak) + jnp.exp2(two - peak), axis=0, keepdims=True)
            peak_r[pl.ds(c, 1), :] = peak
            sum_r[pl.ds(c, 1), :] = total

    def to_line(src, dst, ssem, rsem):
        def send(d, c):
            to = lax.rem(i + lax.rem(d + 6, NS - 1) + 1, NS)
            remote(src, dst, ssem, rsem, (to, k)).start()
            return c

        lax.fori_loop(0, NS - 1, send, 0)

    mine = pl.multiple_of(HALF * core, HALF)
    other = HALF - mine
    mine_z = pl.multiple_of(QUARTER * odd, QUARTER)
    other_z = QUARTER - mine_z
    grouped(extra_first, EXTRA, 8)
    for it in range(ITERS):
        if it > 0:
            cols = columns_of(t_pot, COL_TILES, 1)
            extras(cols, AT, COL_TILES)
            row_half(cols, other)
        half_out[it] = fold(other, HALF, 0)
        remote(half_out.at[it], half_in.at[it], half_send.at[it], half_recv.at[it], (i, sibling)).start()
        if it > 0:
            row_half(cols, mine)
        one = fold(mine, HALF, 0)
        drain(half_in.at[it], half_recv.at[it])
        two = half_in[it]
        top = jnp.maximum(one, two)
        both = top + jnp.log2(jnp.exp2(one - top) + jnp.exp2(two - top))
        if it == 0:
            row_out[...] = both
            row_in[k] = both
            to_plane(row_out, row_in.at[k], row_send.at[0], row_recv.at[0])
            to_line(own_b, b_parts.at[i], mass_send.at[1], mass_recv.at[1])
            grouped(extra_second, EXTRA, 4)
            shards_from(3, 14, fixed_second)
            drain(row_in.at[pl.ds(0, NT - 1)], row_recv.at[0])
            total = lse_leading(row_in[...].reshape(NS, ROW_TILES, TILE))
            drain(a_parts.at[pl.ds(0, NT - 1)], mass_recv.at[0])
            for n in range(NT):
                a_all[2 * n : 2 * n + 2, :] = a_parts[n]
        else:
            rest = (both - row_tot[pl.ds(mine, HALF), :]).astype(jnp.bfloat16)
            row_out16[it - 1] = rest
            row_in16[it - 1, k] = rest
            to_plane(row_out16.at[it - 1], row_in16.at[it - 1, k], row_send.at[it], row_recv.at[it])
            drain(row_in16.at[it - 1, pl.ds(0, NT - 1)], row_recv.at[it])
            parts = row_in16[it - 1].reshape(NS, ROW_TILES, TILE).astype(jnp.float32)
            total = row_tot[...] + lse_leading(parts)
        row_tot[...] = total
        s_pot[...] = a_all[...] - total

        cols = columns_of(s_pot, ROW_TILES, 0)
        extras(cols, A, ROW_TILES)
        if it == 0:
            col_range(cols, other_z, QUARTER)
            pair_out[...] = fold(other_z, QUARTER, 1)
            remote(pair_out, pair_in, pair_sem.at[0], pair_sem.at[1], (partner, k)).start()
            col_range(cols, mine_z, QUARTER)
            one = fold(mine_z, QUARTER, 1)
            drain(b_parts.at[pl.ds(0, NS - 1)], mass_recv.at[1])
            for n in range(NS):
                b_all[2 * n : 2 * n + 2, :] = b_parts[n]
            drain(pair_in, pair_sem.at[1])
            two = pair_in[...]
            top = jnp.maximum(one, two)
            both = top + jnp.log2(jnp.exp2(one - top) + jnp.exp2(two - top))
            col_out[...] = both
            col_in[i] = both
            to_line(col_out, col_in.at[i], col_send.at[0], col_recv.at[0])
            drain(col_in.at[pl.ds(0, NS - 1)], col_recv.at[0])
            total = lse_leading(col_in[...].reshape(NS // 2, COL_TILES, TILE))
        else:
            col_range(cols, 0, COL_TILES)
            logs = fold(0, COL_TILES, 1)
        if 0 < it < ITERS - 1:
            rest = (logs - col_tot[...]).astype(jnp.bfloat16)
            col_out16[...] = rest
            col_in16[i] = rest
            to_line(col_out16, col_in16.at[i], col_send.at[it], col_recv.at[it])
            drain(col_in16.at[pl.ds(0, NS - 1)], col_recv.at[it])
            total = col_tot[...] + lse_leading(col_in16[...].astype(jnp.float32))
        if it + 1 < ITERS:
            col_tot[...] = total
            t_pot[...] = b_all[...] - total
    for n in range(NS):
        fin_out[n] = logs[2 * n : 2 * n + 2]
    fin_in[i] = fin_out[i]

    def send_fin(d, c):
        to = lax.rem(i + lax.rem(d + 6, NS - 1) + 1, NS)
        remote(fin_out.at[to], fin_in.at[i], col_send.at[2], col_recv.at[2], (to, k)).start()
        return c

    lax.fori_loop(0, NS - 1, send_fin, 0)
    pots[0] = s_pot[pl.ds(2 * k, 2), :] * LN2
    drain(Y.at[pl.ds(0, 15)], z_send.at[0])
    drain(Y.at[pl.ds(0, 15)], z_send.at[1])
    drain(X.at[pl.ds(0, 30)], x_send.at[0])
    drain(X.at[pl.ds(0, 32)], x_send.at[1])
    drain(a_parts.at[pl.ds(0, NT - 1)], mass_send.at[0])
    drain(b_parts.at[pl.ds(0, NS - 1)], mass_send.at[1])
    for it in range(ITERS):
        drain(half_in.at[it], half_send.at[it])
    drain(row_in.at[pl.ds(0, NT - 1)], row_send.at[0])
    for it in range(1, ITERS):
        drain(row_in16.at[it - 1, pl.ds(0, NT - 1)], row_send.at[it])
    drain(pair_in, pair_sem.at[0])
    drain(col_in.at[pl.ds(0, NS - 1)], col_send.at[0])
    drain(col_in16.at[pl.ds(0, NS - 1)], col_send.at[1])
    drain(fin_in.at[pl.ds(0, NS - 1)], col_send.at[2])
    drain(fin_in.at[pl.ds(0, NS - 1)], col_recv.at[2])
    pots[1] = (own_b[...] - lse_leading(fin_in[...])) * LN2


def shards(src_points, src_logmass, tgt_points, tgt_logmass, tile_list, tile_count):
    f32, bf16 = jnp.float32, jnp.bfloat16
    vmem = pl.BlockSpec(memory_space=pltpu.VMEM)
    hbm = pl.BlockSpec(memory_space=pltpu.HBM)
    dma = pltpu.SemaphoreType.DMA
    pots = pl.pallas_call(
        kernel,
        out_shape=jax.ShapeDtypeStruct((2, 2, TILE), f32),
        in_specs=[hbm, vmem, hbm, vmem, hbm, hbm],
        out_specs=vmem,
        scratch_shapes=[
            pltpu.SMEM((2, SLOTS), jnp.int32),
            pltpu.SMEM((1, 1), jnp.int32),
            pltpu.VMEM((ROW_TILES, TILE, D), bf16),
            pltpu.VMEM((COL_TILES, TILE, D), bf16),
            pltpu.VMEM((SLOTS, TILE, TILE), f32),
            pltpu.VMEM((SLOTS, TILE, TILE), f32),
            pltpu.VMEM((NT, 2, TILE), f32),
            pltpu.VMEM((NS, 2, TILE), f32),
            pltpu.VMEM((ROW_TILES, TILE), f32),
            pltpu.VMEM((COL_TILES, TILE), f32),
            pltpu.VMEM((2, TILE), f32),
            pltpu.VMEM((2, TILE), f32),
            pltpu.VMEM((ROW_TILES, TILE), f32),
            pltpu.VMEM((ROW_TILES, TILE), f32),
            pltpu.VMEM((EXTRA, TILE), f32),
            pltpu.VMEM((EXTRA, TILE), f32),
            pltpu.VMEM((ROW_TILES, TILE), f32),
            pltpu.VMEM((COL_TILES, TILE), f32),
            pltpu.VMEM((ROW_TILES, TILE), f32),
            pltpu.VMEM((COL_TILES, TILE), f32),
            pltpu.VMEM((ITERS, HALF, TILE), f32),
            pltpu.VMEM((ITERS, HALF, TILE), f32),
            pltpu.VMEM((HALF, TILE), f32),
            pltpu.VMEM((NT, HALF, TILE), f32),
            pltpu.VMEM((ITERS - 1, HALF, TILE), bf16),
            pltpu.VMEM((ITERS - 1, NT, HALF, TILE), bf16),
            pltpu.VMEM((TILE, TILE), f32),
            pltpu.VMEM((QUARTER, TILE), f32),
            pltpu.VMEM((QUARTER, TILE), f32),
            pltpu.VMEM((QUARTER, TILE), f32),
            pltpu.VMEM((NS, QUARTER, TILE), f32),
            pltpu.VMEM((COL_TILES, TILE), bf16),
            pltpu.VMEM((NS, COL_TILES, TILE), bf16),
            pltpu.VMEM((NS, 2, TILE), f32),
            pltpu.VMEM((NS, 2, TILE), f32),
            dma((8 * PIECES,)),
            dma((8 * PIECES,)),
            dma((2,)),
            dma((4,)),
            dma((16,)),
            dma((2,)),
            dma((1,)),
            dma((2,)),
            dma((2,)),
            dma((4,)),
            dma((ITERS,)),
            dma((ITERS,)),
            dma((ITERS,)),
            dma((ITERS,)),
            dma((ITERS,)),
            dma((ITERS,)),
            dma((2,)),
        ],
        compiler_params=pltpu.CompilerParams(
            collective_id=0, has_side_effects=True, vmem_limit_bytes=60 * 2**20
        ),
    )(
        src_points.reshape(2, TILE, D),
        src_logmass,
        tgt_points.reshape(2, TILE, D),
        tgt_logmass,
        tile_list.reshape(SLOTS, 2).T,
        tile_count,
    )
    return pots[0].reshape(1, 2 * TILE), pots[1].reshape(1, 2 * TILE)


def solution(mesh):
    placed = (
        P("src", "tgt", None),
        P("src", "tgt"),
        P("tgt", "src", None),
        P("tgt", "src"),
        P("src", "tgt", None, None),
        P("src", "tgt"),
    )
    return jax.shard_map(
        shards,
        mesh=mesh,
        in_specs=placed,
        out_specs=(P("src", "tgt"), P("tgt", "src")),
        check_vma=False,
    )
```

```python
import math

import jax
import jax.numpy as jnp
from jax import lax
from jax.experimental import pallas as pl
from jax.experimental.pallas import tpu as pltpu
from jax.sharding import PartitionSpec as P

MESH = pl.DeviceIdType.MESH
TILE = 128
D = 256
ROW_TILES = 64
COL_TILES = 32
SLOTS = 80
FIXED = 64
EXTRA = SLOTS - FIXED
ITERS = 3
NS = 16
NT = 32
PIECES = 4
PLANE = sorted(
    ((x, y, c) for x in range(4) for y in range(4) for c in range(2) if x + y + c),
    key=lambda d: -(d[0] % 4 * (4 - d[0]) + d[1] % 4 * (4 - d[1])),
)
PIECE = 2 * TILE // PIECES
QUARTER = COL_TILES // 2
HALF = ROW_TILES // 2
LOG2E = math.log2(math.e)
LN2 = math.log(2.0)
SCALE = -20.0 * LOG2E
LOWEST = -1.0e30
NT_DIMS = (((1,), (1,)), ((), ()))


def scaled_cost(left, right):
    products = lax.dot_general(left, right, NT_DIMS, preferred_element_type=jnp.float32)
    return (1.0 - products).astype(jnp.bfloat16).astype(jnp.float32) * SCALE


def peak_and_sum(scores):
    peak = jnp.max(scores, axis=0, keepdims=True)
    return peak, jnp.sum(jnp.exp2(scores - peak), axis=0, keepdims=True)


def lse_leading(parts):
    peak = jnp.max(parts, axis=0)
    return peak + jnp.log2(jnp.sum(jnp.exp2(parts - peak[None]), axis=0))


def kernel(
    xp, am, yp, bm, tiles_hbm, count_hbm, pots,
    tiles, count,
    X, Y, A, AT, a_parts, b_parts, a_all, b_all, own_a, own_b,
    peak_r, sum_r, peak_x, sum_x, s_pot, t_pot, row_tot, col_tot,
    half_out, half_in, row_out, row_in, row_out16, row_in16,
    spread, pair_out, pair_in, col_out, col_in, col_out16, col_in16, fin_out, fin_in,
    z_up, z_dn, z_send, xa, xb, x_send, sib_recv, mass_recv, mass_send, local,
    half_recv, half_send, row_recv, row_send, col_recv, col_send, pair_sem,
):
    i = lax.axis_index("src")
    k = lax.axis_index("tgt")
    core = lax.rem(k, 2)
    sibling = k + 1 - 2 * core
    up = lax.rem(i + 1, NS)
    dn = lax.rem(i + NS - 1, NS)
    odd = lax.rem(i, 2)
    partner = i + 1 - 2 * odd
    px, py = k // 8, lax.rem(k // 2, 4)
    pa = px * (1 - core) + py * core
    pb = py * (1 - core) + px * core

    def at(da, db):
        a, b = lax.rem(pa + 4 + da, 4), lax.rem(pb + 4 + db, 4)
        return (a * (1 - core) + b * core) * 8 + (b * (1 - core) + a * core) * 2 + core

    barrier = pltpu.get_barrier_semaphore()
    near = ((up, k), (dn, k), (i, at(1, 0)), (i, at(-1, 0)), (i, at(0, 1)), (i, at(0, -1)), (i, sibling))
    for dev in near:
        pl.semaphore_signal(barrier, inc=1, device_id=dev, device_id_type=MESH)
    own_x = pltpu.make_async_copy(xp, X.at[pl.ds(2 * k, 2)], local.at[0])
    own_y = pltpu.make_async_copy(yp, Y.at[pl.ds(2 * i, 2)], local.at[1])
    own_tiles = pltpu.make_async_copy(tiles_hbm, tiles, local.at[2])
    own_count = pltpu.make_async_copy(count_hbm, count, local.at[3])
    for copy in (own_y, own_x, own_tiles, own_count):
        copy.start()
    own_y.wait()
    pl.semaphore_wait(barrier, len(near))

    def remote(src, dst, ssem, rsem, dev):
        return pltpu.make_async_remote_copy(
            src_ref=src, dst_ref=dst, send_sem=ssem, recv_sem=rsem, device_id=dev, device_id_type=MESH
        )

    def drain(like, sem):
        pltpu.make_async_copy(like, like, sem).wait()

    def to_plane(src, dst, ssem, rsem):
        for dx, dy, dc in PLANE:
            to = lax.rem(px + dx, 4) * 8 + lax.rem(py + dy, 4) * 2 + lax.rem(core + dc, 2)
            remote(src, dst, ssem, rsem, (i, to)).start()

    def z_piece(shard, q):
        return Y.at[2 * shard + q // (PIECES // 2), pl.ds((q % (PIECES // 2)) * PIECE, PIECE)]

    def z_copy(shard, q, distance, direction, to):
        block = z_piece(shard, q)
        sem = (z_up, z_dn)[direction].at[(distance - 1) * PIECES + q]
        return remote(block, block, z_send.at[direction], sem, (to, k))

    def z_wait(shard, q, distance, direction):
        drain(z_piece(shard, q), (z_up, z_dn)[direction].at[(distance - 1) * PIECES + q])

    def x_block(da, db):
        return X.at[pl.ds(2 * at(da, db), 2)]

    def x_tile(da, db, t):
        return X.at[2 * at(da, db) + t]

    def x_copy(block, sem, da, db):
        remote(block, block, x_send.at[0], sem, (i, at(da, db))).start()

    def x_sibling(da, db):
        block = x_block(da, db)
        remote(block, block, x_send.at[1], sib_recv.at[0], (i, sibling)).start()

    OFFSETS = (0, -1, 1, 2)

    def x_both(j):
        block = x_block(OFFSETS[j], 0)
        x_copy(block, xb.at[j], 0, 1)
        x_copy(block, xb.at[4 + j], 0, -1)
        x_sibling(OFFSETS[j], 0)

    def x_step(step):
        if step == 1:
            for j, da, tile in ((1, -1, 0), (2, 1, 1)):
                drain(x_block(da, 0), xa.at[j - 1])
                x_copy(x_tile(da, 0, tile), xa.at[1 + j], -da, 0)
                x_both(j)
        if step == 2:
            drain(x_tile(2, 0, 0), xa.at[2])
            drain(x_tile(2, 0, 1), xa.at[3])
            x_both(3)
        for j in {2: (0,), 3: (1, 2), 4: (3,)}.get(step, ()):
            for n, db in ((0, -1), (1, 1)):
                drain(x_block(OFFSETS[j], db), xb.at[4 * n + j])
                x_copy(x_tile(OFFSETS[j], db, n), xb.at[8 + 4 * n + j], 0, -db)
                x_sibling(OFFSETS[j], db)
        for j in {4: (0,), 5: (1, 2, 3)}.get(step, ()):
            for n in range(2):
                drain(x_tile(OFFSETS[j], 2, n), xb.at[8 + 4 * n + j])
            x_sibling(OFFSETS[j], 2)
        if step == 6:
            drain(X.at[pl.ds(0, 2 * NS)], sib_recv.at[0])

    def fixed_first(c):
        pair = jnp.concatenate([X[c], X[c + COL_TILES]], axis=0)
        costs = scaled_cost(Y[c], pair)
        peak, total = peak_and_sum(costs)
        for h in range(2):
            r = c + COL_TILES * h
            AT[r] = costs[:, TILE * h : TILE * (h + 1)]
            peak_r[pl.ds(r, 1), :] = peak[:, TILE * h : TILE * (h + 1)]
            sum_r[pl.ds(r, 1), :] = total[:, TILE * h : TILE * (h + 1)]

    def fixed_second(c):
        for h in range(2):
            r = c + COL_TILES * h
            A[r] = scaled_cost(X[r], Y[c])

    def shards_from(low, high, *bodies):
        def shard(n, carry):
            for half in range(2):
                for body in bodies:
                    body(2 * lax.rem(i + n, NS) + half)
            return carry

        lax.fori_loop(NS + low, NS + high, shard, 0)

    for q in range(PIECES):
        for direction, to in ((0, up), (1, dn)):
            z_copy(i, q, 1, direction, to).start()
    own_x.wait()
    x_copy(x_block(0, 0), xa.at[0], 1, 0)
    x_copy(x_block(0, 0), xa.at[1], -1, 0)
    x_both(0)
    own_tiles.wait()
    own_count.wait()
    spread[...] = jnp.zeros((TILE, TILE), jnp.float32)
    own_a[0:1, :] = am[:, 0:TILE].astype(jnp.float32) * LOG2E
    own_a[1:2, :] = am[:, TILE:].astype(jnp.float32) * LOG2E
    own_b[0:1, :] = bm[:, 0:TILE].astype(jnp.float32) * LOG2E
    own_b[1:2, :] = bm[:, TILE:].astype(jnp.float32) * LOG2E
    a_parts[k] = own_a[...]
    b_parts[i] = own_b[...]
    for step in range(1, 8):
        for q in range(PIECES):
            for direction, shard, to in ((0, lax.rem(i + NS - step, NS), up), (1, lax.rem(i + step, NS), dn)):
                z_wait(shard, q, step, direction)
                if step < 7 or q // (PIECES // 2) == direction:
                    z_copy(shard, q, step + 1, direction, to).start()
        x_step(step)
        if step == 6:
            to_plane(own_a, a_parts.at[k], mass_send.at[0], mass_recv.at[0])
            shards_from(-2, 3, fixed_first, fixed_second)
        if step == 7:
            shards_from(-6, -2, fixed_first)
            shards_from(3, 7, fixed_first)
    far = lax.rem(i + 8, NS)
    for q in range(PIECES):
        z_wait(far, q, 8, q // (PIECES // 2))
    for n in range(7, 10):
        for half in range(2):
            fixed_first(2 * lax.rem(i + n, NS) + half)
    live_count = count[0, 0]

    def alive(s):
        return jnp.full((1, TILE), live_count, jnp.int32) > FIXED + s

    def keep_extra(s, peak, total):
        peak_x[pl.ds(s, 1), :] = jnp.where(alive(s), peak, LOWEST)
        sum_x[pl.ds(s, 1), :] = total

    def row_of(s):
        return tiles[0, FIXED + s]

    def col_of(s):
        return tiles[1, FIXED + s]

    def grouped(body, count, size):
        def group(g, carry):
            for u in range(size):
                body(size * g + u)
            return carry

        lax.fori_loop(0, count // size, group, 0)

    def extra_first(s):
        costs = scaled_cost(Y[col_of(s)], X[row_of(s)])
        AT[FIXED + s] = costs
        keep_extra(s, *peak_and_sum(costs))

    def extra_second(s):
        A[FIXED + s] = scaled_cost(X[row_of(s)], Y[col_of(s)])

    def fold(first, size, which):
        peak = peak_r[pl.ds(first, size), :]
        owner = lax.broadcasted_iota(jnp.int32, (size, TILE), 0) + first
        pick_id = row_of if which == 0 else col_of
        px = peak_x[...]
        sx = sum_x[...]
        highest = peak
        for s in range(EXTRA):
            highest = jnp.maximum(highest, jnp.where(owner == pick_id(s), px[s : s + 1], LOWEST))
        total = sum_r[pl.ds(first, size), :] * jnp.exp2(peak - highest)
        for s in range(EXTRA):
            shortfall = jnp.minimum(px[s : s + 1] - highest, 0.0)
            total = total + jnp.where(owner == pick_id(s), sx[s : s + 1] * jnp.exp2(shortfall), 0.0)
        return highest + jnp.log2(total)

    def columns_of(pot, first, which):
        spread[0:first, :] = pot[...]
        for s in range(EXTRA):
            spread[first + s : first + s + 1, :] = pot[pl.ds(row_of(s) if which == 0 else col_of(s), 1), :]
        return spread[...].T

    def lanes_from(cols, first):
        return cols if isinstance(first, int) else pltpu.roll(cols, lax.rem(TILE - first, TILE), 1)

    def extras(cols, costs, first):
        for g in range(EXTRA // 8):
            for u in range(8):
                s = 8 * g + u
                keep_extra(s, *peak_and_sum(costs[FIXED + s] + cols[:, first + s : first + s + 1]))

    def row_half(cols, first):
        for c in range(HALF):
            peak, total = peak_and_sum(AT[c + first] + cols[:, c : c + 1])
            peak_r[pl.ds(c + first, 1), :] = peak
            sum_r[pl.ds(c + first, 1), :] = total

    def col_range(cols, first, size):
        near = lanes_from(cols, first)
        for u in range(size):
            c = u + first
            one = A[c] + near[:, u : u + 1]
            two = A[c + COL_TILES] + near[:, COL_TILES + u : COL_TILES + u + 1]
            peak = jnp.max(jnp.maximum(one, two), axis=0, keepdims=True)
            total = jnp.sum(jnp.exp2(one - peak) + jnp.exp2(two - peak), axis=0, keepdims=True)
            peak_r[pl.ds(c, 1), :] = peak
            sum_r[pl.ds(c, 1), :] = total

    def to_line(src, dst, ssem, rsem):
        def send(d, c):
            to = lax.rem(i + lax.rem(d + 6, NS - 1) + 1, NS)
            remote(src, dst, ssem, rsem, (to, k)).start()
            return c

        lax.fori_loop(0, NS - 1, send, 0)

    mine = pl.multiple_of(HALF * core, HALF)
    other = HALF - mine
    mine_z = pl.multiple_of(QUARTER * odd, QUARTER)
    other_z = QUARTER - mine_z
    grouped(extra_first, EXTRA, 16)
    for it in range(ITERS):
        if it > 0:
            cols = columns_of(t_pot, COL_TILES, 1)
            extras(cols, AT, COL_TILES)
            row_half(cols, other)
        half_out[it] = fold(other, HALF, 0)
        remote(half_out.at[it], half_in.at[it], half_send.at[it], half_recv.at[it], (i, sibling)).start()
        if it > 0:
            row_half(cols, mine)
        one = fold(mine, HALF, 0)
        drain(half_in.at[it], half_recv.at[it])
        two = half_in[it]
        top = jnp.maximum(one, two)
        both = top + jnp.log2(jnp.exp2(one - top) + jnp.exp2(two - top))
        if it == 0:
            row_out[...] = both
            row_in[k] = both
            to_plane(row_out, row_in.at[k], row_send.at[0], row_recv.at[0])
            to_line(own_b, b_parts.at[i], mass_send.at[1], mass_recv.at[1])
            grouped(extra_second, EXTRA, 4)
            shards_from(3, 14, fixed_second)
            drain(a_parts.at[pl.ds(0, NT - 1)], mass_recv.at[0])
            for n in range(NT):
                a_all[2 * n : 2 * n + 2, :] = a_parts[n]
            drain(row_in.at[pl.ds(0, NT - 1)], row_recv.at[0])
            total = lse_leading(row_in[...].reshape(NS, ROW_TILES, TILE))
        else:
            rest = (both - row_tot[pl.ds(mine, HALF), :]).astype(jnp.bfloat16)
            row_out16[it - 1] = rest
            row_in16[it - 1, k] = rest
            to_plane(row_out16.at[it - 1], row_in16.at[it - 1, k], row_send.at[it], row_recv.at[it])
            drain(row_in16.at[it - 1, pl.ds(0, NT - 1)], row_recv.at[it])
            parts = row_in16[it - 1].reshape(NS, ROW_TILES, TILE).astype(jnp.float32)
            total = row_tot[...] + lse_leading(parts)
        row_tot[...] = total
        s_pot[...] = a_all[...] - total

        cols = columns_of(s_pot, ROW_TILES, 0)
        extras(cols, A, ROW_TILES)
        if it == 0:
            col_range(cols, other_z, QUARTER)
            pair_out[...] = fold(other_z, QUARTER, 1)
            remote(pair_out, pair_in, pair_sem.at[0], pair_sem.at[1], (partner, k)).start()
            col_range(cols, mine_z, QUARTER)
            one = fold(mine_z, QUARTER, 1)
            drain(b_parts.at[pl.ds(0, NS - 1)], mass_recv.at[1])
            for n in range(NS):
                b_all[2 * n : 2 * n + 2, :] = b_parts[n]
            drain(pair_in, pair_sem.at[1])
            two = pair_in[...]
            top = jnp.maximum(one, two)
            both = top + jnp.log2(jnp.exp2(one - top) + jnp.exp2(two - top))
            col_out[...] = both
            col_in[i] = both
            to_line(col_out, col_in.at[i], col_send.at[0], col_recv.at[0])
            drain(col_in.at[pl.ds(0, NS - 1)], col_recv.at[0])
            total = lse_leading(col_in[...].reshape(NS // 2, COL_TILES, TILE))
        else:
            col_range(cols, 0, COL_TILES)
            logs = fold(0, COL_TILES, 1)
        if 0 < it < ITERS - 1:
            rest = (logs - col_tot[...]).astype(jnp.bfloat16)
            col_out16[...] = rest
            col_in16[i] = rest
            to_line(col_out16, col_in16.at[i], col_send.at[it], col_recv.at[it])
            drain(col_in16.at[pl.ds(0, NS - 1)], col_recv.at[it])
            total = col_tot[...] + lse_leading(col_in16[...].astype(jnp.float32))
        if it + 1 < ITERS:
            col_tot[...] = total
            t_pot[...] = b_all[...] - total
    for n in range(NS):
        fin_out[n] = logs[2 * n : 2 * n + 2]
    fin_in[i] = fin_out[i]

    def send_fin(d, c):
        to = lax.rem(i + lax.rem(d + 6, NS - 1) + 1, NS)
        remote(fin_out.at[to], fin_in.at[i], col_send.at[2], col_recv.at[2], (to, k)).start()
        return c

    lax.fori_loop(0, NS - 1, send_fin, 0)
    pots[0] = s_pot[pl.ds(2 * k, 2), :] * LN2
    drain(Y.at[pl.ds(0, 15)], z_send.at[0])
    drain(Y.at[pl.ds(0, 15)], z_send.at[1])
    drain(X.at[pl.ds(0, 30)], x_send.at[0])
    drain(X.at[pl.ds(0, 32)], x_send.at[1])
    drain(a_parts.at[pl.ds(0, NT - 1)], mass_send.at[0])
    drain(b_parts.at[pl.ds(0, NS - 1)], mass_send.at[1])
    for it in range(ITERS):
        drain(half_in.at[it], half_send.at[it])
    drain(row_in.at[pl.ds(0, NT - 1)], row_send.at[0])
    for it in range(1, ITERS):
        drain(row_in16.at[it - 1, pl.ds(0, NT - 1)], row_send.at[it])
    drain(pair_in, pair_sem.at[0])
    drain(col_in.at[pl.ds(0, NS - 1)], col_send.at[0])
    drain(col_in16.at[pl.ds(0, NS - 1)], col_send.at[1])
    drain(fin_in.at[pl.ds(0, NS - 1)], col_send.at[2])
    drain(fin_in.at[pl.ds(0, NS - 1)], col_recv.at[2])
    pots[1] = (own_b[...] - lse_leading(fin_in[...])) * LN2


def shards(src_points, src_logmass, tgt_points, tgt_logmass, tile_list, tile_count):
    f32, bf16 = jnp.float32, jnp.bfloat16
    vmem = pl.BlockSpec(memory_space=pltpu.VMEM)
    hbm = pl.BlockSpec(memory_space=pltpu.HBM)
    dma = pltpu.SemaphoreType.DMA
    pots = pl.pallas_call(
        kernel,
        out_shape=jax.ShapeDtypeStruct((2, 2, TILE), f32),
        in_specs=[hbm, vmem, hbm, vmem, hbm, hbm],
        out_specs=vmem,
        scratch_shapes=[
            pltpu.SMEM((2, SLOTS), jnp.int32),
            pltpu.SMEM((1, 1), jnp.int32),
            pltpu.VMEM((ROW_TILES, TILE, D), bf16),
            pltpu.VMEM((COL_TILES, TILE, D), bf16),
            pltpu.VMEM((SLOTS, TILE, TILE), f32),
            pltpu.VMEM((SLOTS, TILE, TILE), f32),
            pltpu.VMEM((NT, 2, TILE), f32),
            pltpu.VMEM((NS, 2, TILE), f32),
            pltpu.VMEM((ROW_TILES, TILE), f32),
            pltpu.VMEM((COL_TILES, TILE), f32),
            pltpu.VMEM((2, TILE), f32),
            pltpu.VMEM((2, TILE), f32),
            pltpu.VMEM((ROW_TILES, TILE), f32),
            pltpu.VMEM((ROW_TILES, TILE), f32),
            pltpu.VMEM((EXTRA, TILE), f32),
            pltpu.VMEM((EXTRA, TILE), f32),
            pltpu.VMEM((ROW_TILES, TILE), f32),
            pltpu.VMEM((COL_TILES, TILE), f32),
            pltpu.VMEM((ROW_TILES, TILE), f32),
            pltpu.VMEM((COL_TILES, TILE), f32),
            pltpu.VMEM((ITERS, HALF, TILE), f32),
            pltpu.VMEM((ITERS, HALF, TILE), f32),
            pltpu.VMEM((HALF, TILE), f32),
            pltpu.VMEM((NT, HALF, TILE), f32),
            pltpu.VMEM((ITERS - 1, HALF, TILE), bf16),
            pltpu.VMEM((ITERS - 1, NT, HALF, TILE), bf16),
            pltpu.VMEM((TILE, TILE), f32),
            pltpu.VMEM((QUARTER, TILE), f32),
            pltpu.VMEM((QUARTER, TILE), f32),
            pltpu.VMEM((QUARTER, TILE), f32),
            pltpu.VMEM((NS, QUARTER, TILE), f32),
            pltpu.VMEM((COL_TILES, TILE), bf16),
            pltpu.VMEM((NS, COL_TILES, TILE), bf16),
            pltpu.VMEM((NS, 2, TILE), f32),
            pltpu.VMEM((NS, 2, TILE), f32),
            dma((8 * PIECES,)),
            dma((8 * PIECES,)),
            dma((2,)),
            dma((4,)),
            dma((16,)),
            dma((2,)),
            dma((1,)),
            dma((2,)),
            dma((2,)),
            dma((4,)),
            dma((ITERS,)),
            dma((ITERS,)),
            dma((ITERS,)),
            dma((ITERS,)),
            dma((ITERS,)),
            dma((ITERS,)),
            dma((2,)),
        ],
        compiler_params=pltpu.CompilerParams(
            collective_id=0, has_side_effects=True, vmem_limit_bytes=60 * 2**20
        ),
    )(
        src_points.reshape(2, TILE, D),
        src_logmass,
        tgt_points.reshape(2, TILE, D),
        tgt_logmass,
        tile_list.reshape(SLOTS, 2).T,
        tile_count,
    )
    return pots[0].reshape(1, 2 * TILE), pots[1].reshape(1, 2 * TILE)


def solution(mesh):
    placed = (
        P("src", "tgt", None),
        P("src", "tgt"),
        P("tgt", "src", None),
        P("tgt", "src"),
        P("src", "tgt", None, None),
        P("src", "tgt"),
    )
    return jax.shard_map(
        shards,
        mesh=mesh,
        in_specs=placed,
        out_specs=(P("src", "tgt"), P("tgt", "src")),
        check_vma=False,
    )
```
